32 devices in a mesh: lev: 4 (over y, x), wave: 8 (over z, core).
Axes of the slice: x: 2, y: 2, z: 4, core: 2. Of those that a mesh axis runs over, the one named last changes fastest.
Arguments:
- spectral: bfloat16 [128, 64, 3, 2, 64], P('lev', 'wave'), may hold values from -6 to 6
- modes_in: bfloat16 [128, 128], replicated, may hold values from -0.5 to 0.5
- modes_out: bfloat16 [128, 128], replicated, may hold values from -0.5 to 0.5
- mode_depth: float32 [128], replicated, may hold values from 0.1 to 10
- legendre: bfloat16 [64, 64, 32], P('wave'), may hold values from -0.75 to 0.75
- wave_map: int32 [64], replicated, may hold values from 0 to 63, as said below
- row_points: int32 [32], P('wave'), may hold values from 320 to 1280, as said below
Outputs:
- advected: float32 [3, 128, 32, 1280], P(None, 'lev', 'wave')
The draws below stay inside these ranges and needn't reach their ends.
Inputs may be any that keep to these rules, and one draw needn't show every extreme that they name: `wave_map`: a permutation of 0 to 63; the entries at slots 2 k and 2 k + 1 add up to 63. `row_points`: some row has all 1280 points.
All inputs are finite; a program needn't handle non-finite values.
Results may differ from the reference program's by a relative error of at most 0.0059.
Values may be sent and summed in bfloat16 or wider, within the bound.
A program may use at most 64 MiB of HBM per device.

```python
import math
import jax
import jax.numpy as jnp
from jax import lax

LEVELS = 128
FIELDS = 3
LON = 1280
M_TOTAL = 64
LAT = 32


def draw_wave_map(key, part):
    shuffled = jax.random.permutation(jax.random.fold_in(key, 7), M_TOTAL // 2).astype(jnp.int32)
    lower_half = shuffled
    upper_half = M_TOTAL - 1 - shuffled
    return jnp.stack([lower_half, upper_half], axis=1).reshape(M_TOTAL).astype(jnp.int32)


def draw_row_points(key, part):
    first_key = jax.random.fold_in(key, 11)
    second_key = jax.random.fold_in(key, 12)
    row_counts = jax.random.randint(first_key, (LAT,), LON // 4, LON + 1, dtype=jnp.int32)
    widest = jax.random.randint(second_key, (), 0, LAT, dtype=jnp.int32)
    return jnp.where(jnp.arange(LAT, dtype=jnp.int32) == widest, LON, row_counts).astype(jnp.int32)


def levels(rng, dims, shards, least, high):
    level = 1.0
    for dim, parts in shards:
        draws = jax.random.uniform(jax.random.fold_in(jax.random.fold_in(rng, 6), dim), (parts,), jnp.float32, least / len(shards), high / len(shards))
        level = level * jnp.repeat(jnp.exp(draws), dims[dim] // parts).reshape((-1,) + (1,) * (len(dims) - 1 - dim))
    return level


def normal_values(stream_key, extent, deviation, reach, split=(), kind=jnp.bfloat16):
    array = deviation * jax.random.normal(stream_key, extent, jnp.float32)
    if split:
        array = array * levels(stream_key, extent, split, -0.22, 0.18)
    return jnp.clip(array, -reach, reach).astype(kind)


def setup_inputs(seed: int = 0) -> dict:
    streams_of = jax.random.split(jax.random.key(seed), 8)
    spectral = normal_values(streams_of[0], (LEVELS, M_TOTAL, FIELDS, 2, M_TOTAL), 1.0, 6.0, ((0, 4), (1, 8)))
    modes_in = normal_values(streams_of[1], (LEVELS, LEVELS), LEVELS ** -0.5, 0.5)
    modes_out = normal_values(streams_of[2], (LEVELS, LEVELS), LEVELS ** -0.5, 0.5)
    mode_depth = jnp.clip(jnp.exp(jax.random.uniform(streams_of[3], (LEVELS,), jnp.float32, math.log(0.1), math.log(10.0))), 0.1, 10.0)
    legendre = normal_values(streams_of[4], (M_TOTAL, M_TOTAL, LAT), M_TOTAL ** -0.5, 0.75, ((0, 8),))
    wave_map = draw_wave_map(jax.random.fold_in(streams_of[7], 71), 0)
    row_points = draw_row_points(jax.random.fold_in(streams_of[7], 71), 0)
    return dict(spectral=spectral, modes_in=modes_in, modes_out=modes_out, mode_depth=mode_depth, legendre=legendre, wave_map=wave_map, row_points=row_points)


time_step = 0.8

def damping(mode_depth, degree_of, degree_total):
    ratio = degree_of * (degree_of + 1.0) / float(degree_total * degree_total)
    return 1.0 / (1.0 + mode_depth[:, None] * ratio[None, :])

def trig_table(wave_map, lon_count):
    column = jnp.arange(lon_count, dtype=jnp.int32)
    product = wave_map[:, None] * column[None, :] % lon_count
    angles = product.astype(jnp.float32) * (2.0 * math.pi / lon_count)
    return jnp.stack([jnp.cos(angles), -jnp.sin(angles)], axis=1).astype(jnp.bfloat16)

def tendency(fields_ext):
    center = fields_ext[..., 1:-1, :]
    ahead_lon = jnp.roll(center, -1, axis=-1)
    behind_lon = jnp.roll(center, 1, axis=-1)
    ahead_lat = fields_ext[..., 2:, :]
    behind_lat = fields_ext[..., :-2, :]
    return center[0] * (ahead_lon - behind_lon) * 0.5 + center[1] * (ahead_lat - behind_lat) * 0.5

def pad_rows(values):
    return jnp.pad(values, ((0, 0), (1, 1), (0, 0)))

def reference(spectral, modes_in, modes_out, mode_depth, legendre, wave_map, row_points):
    degrees = jnp.arange(M_TOTAL, dtype=jnp.int32)
    keep_mask = degrees[None, :] >= wave_map[:, None]
    masked = jnp.where(keep_mask[None, :, None, None, :], spectral, jnp.zeros_like(spectral))
    flattened = masked.reshape(LEVELS, -1)
    modal_part = jnp.dot(modes_in, flattened, preferred_element_type=jnp.float32)
    degree_of = (jnp.arange(flattened.shape[1], dtype=jnp.int32) % M_TOTAL).astype(jnp.float32)
    scaled = (modal_part * damping(mode_depth, degree_of, M_TOTAL)).astype(jnp.bfloat16)
    solved = jnp.dot(modes_out, scaled, preferred_element_type=jnp.float32).astype(jnp.bfloat16)
    solved = solved.reshape(spectral.shape)
    trig_rows = trig_table(wave_map, LON).astype(jnp.float32)
    legendre_wide = legendre.astype(jnp.float32)
    points = jnp.arange(LON, dtype=jnp.int32)[None, :] < row_points[:, None]
    norm_factor = 1.0 / math.sqrt(M_TOTAL)

    def one_level(level_coef):
        band_rows = jnp.einsum('sfcn,snt->tsfc', level_coef.astype(jnp.float32), legendre_wide, precision=lax.Precision.HIGHEST).astype(jnp.bfloat16)
        grid_field = jnp.einsum('tsfc,scx->ftx', band_rows.astype(jnp.float32), trig_rows, precision=lax.Precision.HIGHEST) * norm_factor
        section_one = grid_field - time_step * tendency(pad_rows(grid_field))
        second = 0.5 * (grid_field + section_one - time_step * tendency(pad_rows(section_one)))
        return jnp.where(points[None, :, :], second, jnp.zeros_like(second))
    result = lax.map(one_level, solved)
    return jnp.transpose(result, (1, 0, 2, 3))
```

```python
import functools
import math

import jax
import jax.numpy as jnp
from jax import lax
from jax.experimental import pallas as pl
from jax.experimental.pallas import tpu as pltpu
from jax.sharding import PartitionSpec as P

LON = 1280


time_step = 0.8


def with_halo(value, sides, width):
    for axis, dim in sides:
        size, length = (lax.axis_size(axis), value.shape[dim])
        up = [(i, (i + 1) % size) for i in range(size - 1)]
        down = [(j, i) for i, j in up]
        last = lax.slice_in_dim(value, length - width, length, axis=dim)
        leading = lax.slice_in_dim(value, 0, width, axis=dim)
        before = lax.ppermute(last, axis, up)
        after = lax.ppermute(leading, axis, down)
        value = jnp.concatenate([before, value, after], axis=dim)
    return value


def damping(mode_depth, degree_of, degree_total):
    ratio = degree_of * (degree_of + 1.0) / float(degree_total * degree_total)
    return 1.0 / (1.0 + mode_depth[:, None] * ratio[None, :])


def trig_table(wave_map, lon_count):
    column = jnp.arange(lon_count, dtype=jnp.int32)
    product = wave_map[:, None] * column[None, :] % lon_count
    angles = product.astype(jnp.float32) * (2.0 * math.pi / lon_count)
    return jnp.stack([jnp.cos(angles), -jnp.sin(angles)], axis=1).astype(jnp.bfloat16)


def tendency(fields_ext):
    center = fields_ext[..., 1:-1, :]
    ahead_lon = jnp.roll(center, -1, axis=-1)
    behind_lon = jnp.roll(center, 1, axis=-1)
    ahead_lat = fields_ext[..., 2:, :]
    behind_lat = fields_ext[..., :-2, :]
    return center[0] * (ahead_lon - behind_lon) * 0.5 + center[1] * (ahead_lat - behind_lat) * 0.5


def legendre_rows(solved, legendre):
    band_rows = jnp.einsum(
        "lsfcn,snt->tlsfc", solved, legendre, preferred_element_type=jnp.float32
    ).astype(jnp.bfloat16)
    return band_rows.reshape(band_rows.shape[0], -1)


def general_path(spectral, modes_in, modes_out, mode_depth, legendre, wave_map, row_points):
    lev_rows = spectral.shape[0]
    wave_slots = spectral.shape[1]
    field_count = spectral.shape[2]
    degree_count = spectral.shape[4]
    shard_count = lax.axis_size("wave")
    first_slot = lax.axis_index("wave") * wave_slots
    local_waves = lax.dynamic_slice_in_dim(wave_map, first_slot, wave_slots)
    degrees = jnp.arange(degree_count, dtype=jnp.int32)
    keep_mask = degrees[None, :] >= local_waves[:, None]
    masked = jnp.where(keep_mask[None, :, None, None, :], spectral, jnp.zeros_like(spectral))
    flattened = masked.reshape(lev_rows, -1)
    trig_rows = trig_table(wave_map, LON).reshape(shard_count, wave_slots, 2, LON)
    norm_factor = 1.0 / math.sqrt(wave_map.shape[0])
    modal_part = jnp.dot(
        modes_in,
        lax.all_gather(flattened, "lev", axis=0, tiled=True),
        preferred_element_type=jnp.float32,
    )
    degree_of = (jnp.arange(flattened.shape[1], dtype=jnp.int32) % degree_count).astype(jnp.float32)
    scaled = (modal_part * damping(mode_depth, degree_of, degree_count)).astype(jnp.bfloat16)
    own_rows = lax.dynamic_slice_in_dim(modes_out, lax.axis_index("lev") * lev_rows, lev_rows, 0)
    solved = jnp.dot(own_rows, scaled, preferred_element_type=jnp.float32).astype(jnp.bfloat16)
    band_rows = legendre_rows(solved.reshape(spectral.shape), legendre)
    regrouped = lax.all_to_all(band_rows, "wave", split_axis=0, concat_axis=1, tiled=True)
    lat_rows = regrouped.shape[0]
    split_bands = regrouped.reshape(lat_rows, shard_count, lev_rows, wave_slots, field_count, 2)
    grid_field = (
        jnp.einsum("twlsfc,wscx->fltx", split_bands, trig_rows, preferred_element_type=jnp.float32)
        * norm_factor
    )
    wide_rows = with_halo(grid_field, (("wave", 2),), 2)
    section_wide = wide_rows[:, :, 1:-1, :] - time_step * tendency(wide_rows)
    second = 0.5 * (grid_field + section_wide[:, :, 1:-1, :] - time_step * tendency(section_wide))
    points = jnp.arange(LON, dtype=jnp.int32)[None, :] < row_points[:, None]
    return jnp.where(points[None, None, :, :], second, jnp.zeros_like(second))


def iota(shape, dim):
    return lax.broadcasted_iota(jnp.int32, shape, dim)


def trig_rows_of(waves, points):
    rows = waves.shape[0]
    column = iota((rows, points), 1).astype(jnp.float32)
    shift = (iota((rows, points), 0) % 2).astype(jnp.float32) * (points / 4)
    product = waves * column + shift
    turns = product * (1.0 / points)
    left = product - jnp.floor(turns) * points
    folded = 0.25 - jnp.abs(left * (1.0 / points) - 0.5)
    angle = folded * (2.0 * math.pi)
    square = angle * angle
    total = jnp.full_like(angle, -1.0 / math.factorial(11))
    for order in (9, 7, 5, 3, 1):
        sign = 1.0 if order % 4 == 1 else -1.0
        total = total * square + sign / math.factorial(order)
    return -(total * angle)


def exchange_kernel(
    dims, x_ref, min_ref, mout_ref, depth_ref, leg_ref, wm_ref,
    bands_ref, table_ref,
    levels_buf, send_buf, recv_buf, wide, lhs, own_sem, lev_send, lev_recv, all_send, all_recv,
):
    groups, shards, slots, lev_rows, fields, degrees, lat_total, scale = dims
    halo_rows = 8
    lat_rows = lat_total // shards
    part_slots = slots // groups
    everyone = groups * shards
    q = lax.axis_index("lev")
    w = lax.axis_index("wave")
    me = w * groups + q

    def coords(place):
        return (lax.rem(place, groups), lax.div(place, groups))

    barrier = pltpu.get_barrier_semaphore()

    def greet(step, carry):
        place = lax.rem(me + step, everyone)
        pl.semaphore_signal(barrier, inc=1, device_id=coords(place), device_id_type=pl.DeviceIdType.MESH)
        return carry

    lax.fori_loop(1, everyone, greet, 0)

    own = pltpu.make_async_copy(x_ref.at[q], levels_buf.at[q], own_sem.at[0])
    own.start()

    total_slots = shards * slots
    wm = wm_ref[...].astype(jnp.float32)
    pair = 2 * degrees
    halo_total = shards * halo_rows
    row = iota((halo_total, lat_total), 0)
    inner = row % halo_rows
    lat = (row // halo_rows) * lat_rows + jnp.where(inner < halo_rows - 2, inner, inner - halo_rows)
    pick = (lat == iota((halo_total, lat_total), 1)).astype(jnp.float32).astype(jnp.bfloat16)
    double = (iota((degrees, pair), 0) == iota((degrees, pair), 1) % degrees)
    double = double.astype(jnp.float32).astype(jnp.bfloat16)
    lane = iota((halo_total, pair), 1)
    degree = (lane % degrees).astype(jnp.float32)
    legs = []
    for s in range(part_slots):
        leg = jnp.dot(leg_ref[q * part_slots + s], double, preferred_element_type=jnp.float32)
        leg = jnp.dot(pick, leg.astype(jnp.bfloat16), preferred_element_type=jnp.float32)
        place = w * slots + q * part_slots + s
        chosen = iota((1, total_slots), 1) == place
        wave = jnp.sum(jnp.where(chosen, wm, 0.0), axis=1, keepdims=True)
        leg = jnp.where(degree >= wave, leg, 0.0)
        both = [jnp.where(lane < degrees, leg, 0.0), jnp.where(lane >= degrees, leg, 0.0)]
        legs.append(jnp.concatenate(both, axis=0).astype(jnp.bfloat16))
    modes = min_ref.shape[0]
    square = (modes, modes)
    eye = iota(square, 0) == iota(square, 1)
    depth = jnp.sum(jnp.where(eye, depth_ref[...], 0.0), axis=1, keepdims=True)
    degree_row = (iota((modes, pair), 1) % degrees).astype(jnp.float32)
    ratio = degree_row * (degree_row + 1.0) / float(degrees * degrees)
    damp = 1.0 / (1.0 + depth * ratio)

    pl.semaphore_wait(barrier, everyone - 1)

    def lev_copy(step):
        peer = lax.rem(q + step, groups)
        return pltpu.make_async_remote_copy(
            src_ref=x_ref.at[peer], dst_ref=levels_buf.at[q],
            send_sem=lev_send.at[peer], recv_sem=lev_recv.at[q],
            device_id=(peer, w), device_id_type=pl.DeviceIdType.MESH,
        )

    for step in range(1, groups):
        lev_copy(step).start()

    rows = 2 * total_slots
    chosen = iota((rows, total_slots), 0) // 2 == iota((rows, total_slots), 1)
    waves = jnp.sum(jnp.where(chosen, wm, 0.0), axis=1, keepdims=True)
    table_ref[...] = (trig_rows_of(waves, table_ref.shape[1]) * scale).astype(jnp.bfloat16)

    own.wait()
    for step in range(1, groups):
        peer = lax.rem(q + step, groups)
        pltpu.make_async_remote_copy(
            src_ref=x_ref.at[peer], dst_ref=levels_buf.at[peer],
            send_sem=lev_send.at[peer], recv_sem=lev_recv.at[peer],
            device_id=(peer, w), device_id_type=pl.DeviceIdType.MESH,
        ).wait_recv()

    columns = levels_buf.shape[2]
    level_count = groups * lev_rows
    coef = levels_buf[...].reshape(level_count, columns)
    modal = jnp.dot(min_ref[...], coef, preferred_element_type=jnp.float32)
    scaled = jnp.concatenate(
        [modal[:, i * pair : (i + 1) * pair] * damp for i in range(columns // pair)], axis=1
    ).astype(jnp.bfloat16)
    solved = jnp.dot(mout_ref[...], scaled, preferred_element_type=jnp.float32).astype(jnp.bfloat16)
    width = send_buf.shape[2]
    spare = jnp.zeros((width - fields * lev_rows, pair), jnp.bfloat16)
    for to in range(groups):
        outs = []
        for s in range(part_slots):
            pieces = []
            for f in range(fields):
                at = (s * fields + f) * pair
                pieces.append(solved[to * lev_rows : (to + 1) * lev_rows, at : at + pair])
            stack = jnp.concatenate(pieces + [spare], axis=0)
            outs.append(lax.dot_general(
                legs[s], stack, (((1,), (1,)), ((), ())), preferred_element_type=jnp.float32
            ))
        for shard in range(shards):
            message = []
            for s in range(part_slots):
                for c in range(2):
                    at = (c * shards + shard) * halo_rows
                    message.append(outs[s][at : at + halo_rows])
            send_buf[shard * groups + to] = jnp.concatenate(message, axis=0).astype(jnp.bfloat16)

    def all_copy(peer, land):
        return pltpu.make_async_remote_copy(
            src_ref=send_buf.at[peer], dst_ref=recv_buf.at[land],
            send_sem=all_send.at[peer], recv_sem=all_recv.at[land],
            device_id=coords(peer), device_id_type=pl.DeviceIdType.MESH,
        )

    def start(step, carry):
        all_copy(lax.rem(me + step, everyone), me).start()
        return carry

    lax.fori_loop(1, everyone, start, 0)
    mine = pltpu.make_async_copy(send_buf.at[me], recv_buf.at[me], own_sem.at[1])
    mine.start()
    mine.wait()

    def finish(step, carry):
        peer = lax.rem(me + step, everyone)
        all_copy(peer, peer).wait_recv()
        return carry

    lax.fori_loop(1, everyone, finish, 0)
    for t in range(0, everyone, 8):
        part = recv_buf[t : t + 8]
        wide[t * part.shape[1] : (t + 8) * part.shape[1]] = part.reshape(-1, width).astype(jnp.float32)
    used = fields * lev_rows
    for t in range(halo_rows):
        rows_t = wide[pl.ds(t, rows, stride=halo_rows), :]
        lhs[pl.ds(t, used, stride=halo_rows), :] = rows_t.T[:used]
    bands_ref[...] = lhs[...].astype(jnp.bfloat16)

    def sent(step, carry):
        all_copy(lax.rem(me + step, everyone), me).wait_send()
        return carry

    lax.fori_loop(1, everyone, sent, 0)
    for step in range(1, groups):
        lev_copy(step).wait_send()


def section_kernel(scale, points_ref, bands_ref, table_ref, out_ref, grid_buf):
    fields, chunk, halo_rows, depth = bands_ref.shape
    lat_rows, width = out_ref.shape[2], out_ref.shape[3]
    table = table_ref[...]
    for f in range(fields):
        part = bands_ref[f].reshape(chunk * halo_rows, depth)
        value = jnp.dot(part, table, preferred_element_type=jnp.float32)
        grid_buf[f] = (value if scale is None else value * scale).reshape(chunk, halo_rows, width)
    row = iota((halo_rows, width), 0)
    limit = jnp.zeros((halo_rows, width), jnp.int32)
    for t in range(lat_rows):
        limit = jnp.where(row == t, points_ref[t], limit)
    keep = iota((halo_rows, width), 1) < limit

    def slopes(value):
        lon = pltpu.roll(value, width - 1, 1) - pltpu.roll(value, 1, 1)
        lat = pltpu.roll(value, halo_rows - 1, 0) - pltpu.roll(value, 1, 0)
        return lon, lat

    def level(i, carry):
        grid = [grid_buf[f, i] for f in range(fields)]
        east, north = grid[0] * (0.5 * time_step), grid[1] * (0.5 * time_step)
        first = []
        for value in grid:
            lon, lat = slopes(value)
            first.append(value - (east * lon + north * lat))
        east, north = first[0] * (0.25 * time_step), first[1] * (0.25 * time_step)
        for f in range(fields):
            lon, lat = slopes(first[f])
            second = 0.5 * (grid[f] + first[f]) - (east * lon + north * lat)
            out_ref[f, i] = jnp.where(keep, second, 0.0)[:lat_rows]
        return carry

    lax.fori_loop(0, chunk, level, 0)


def per_device(spectral, modes_in, modes_out, mode_depth, legendre, wave_map, row_points):
    lev_rows, slots, fields, _, degrees = spectral.shape
    groups, shards = lax.axis_size("lev"), lax.axis_size("wave")
    lat_total = legendre.shape[2]
    lat_rows = lat_total // shards
    used = fields * lev_rows
    fits = slots % groups == 0 and 2 * degrees == 128 and lat_rows == 4 and used <= 128
    fits = fits and lev_rows % 16 == 0 and (groups * shards) % 8 == 0 and 2 * shards * slots == 128
    if not fits:
        return general_path(spectral, modes_in, modes_out, mode_depth, legendre, wave_map, row_points)
    everyone, halo_rows, width = groups * shards, 8, 128
    part_slots = slots // groups
    rows = 2 * shards * slots
    norm = 1.0 / math.sqrt(shards * slots)
    exact = math.frexp(norm)[0] == 0.5
    columns = part_slots * fields * 2 * degrees
    x = spectral.reshape(lev_rows, groups, columns).transpose(1, 0, 2)
    dims = (groups, shards, slots, lev_rows, fields, degrees, lat_total, norm if exact else 1.0)
    vmem = pl.BlockSpec(memory_space=pltpu.VMEM)
    message = part_slots * 2 * halo_rows
    bands, table = pl.pallas_call(
        functools.partial(exchange_kernel, dims),
        out_shape=(
            jax.ShapeDtypeStruct((used * halo_rows, rows), jnp.bfloat16),
            jax.ShapeDtypeStruct((rows, LON), jnp.bfloat16),
        ),
        in_specs=[vmem] * 6,
        out_specs=(vmem, vmem),
        scratch_shapes=[
            pltpu.VMEM((groups, lev_rows, columns), jnp.bfloat16),
            pltpu.VMEM((everyone, message, width), jnp.bfloat16),
            pltpu.VMEM((everyone, message, width), jnp.bfloat16),
            pltpu.VMEM((everyone * message, width), jnp.float32),
            pltpu.VMEM((used * halo_rows, rows), jnp.float32),
            pltpu.SemaphoreType.DMA((2,)),
            pltpu.SemaphoreType.DMA((groups,)),
            pltpu.SemaphoreType.DMA((groups,)),
            pltpu.SemaphoreType.DMA((everyone,)),
            pltpu.SemaphoreType.DMA((everyone,)),
        ],
        compiler_params=pltpu.CompilerParams(
            collective_id=0, has_side_effects=True, vmem_limit_bytes=32 * 1024 * 1024
        ),
        name="exchange",
    )(
        x, modes_in, modes_out, mode_depth.reshape(1, -1),
        jnp.swapaxes(legendre, 1, 2), wave_map.reshape(1, -1),
    )
    chunk = 8
    return pl.pallas_call(
        functools.partial(section_kernel, None if exact else norm),
        grid=(lev_rows // chunk,),
        out_shape=jax.ShapeDtypeStruct((fields, lev_rows, lat_rows, LON), jnp.float32),
        in_specs=[
            pl.BlockSpec(memory_space=pltpu.SMEM),
            pl.BlockSpec((fields, chunk, halo_rows, rows), lambda i: (0, i, 0, 0)),
            pl.BlockSpec((rows, LON), lambda i: (0, 0)),
        ],
        out_specs=pl.BlockSpec((fields, chunk, lat_rows, LON), lambda i: (0, i, 0, 0)),
        scratch_shapes=[pltpu.VMEM((fields, chunk, halo_rows, LON), jnp.float32)],
        compiler_params=pltpu.CompilerParams(vmem_limit_bytes=32 * 1024 * 1024),
        name="sections",
    )(row_points, bands.reshape(fields, lev_rows, halo_rows, rows), table)


def solution(mesh):
    in_specs = (
        P("lev", "wave", None, None, None),
        P(),
        P(),
        P(),
        P("wave", None, None),
        P(),
        P("wave"),
    )
    out_specs = P(None, "lev", "wave", None)
    return jax.shard_map(
        per_device, mesh=mesh, in_specs=in_specs, out_specs=out_specs, check_vma=False
    )
```

```python
import functools
import math

import jax
import jax.numpy as jnp
from jax import lax
from jax.experimental import pallas as pl
from jax.experimental.pallas import tpu as pltpu
from jax.sharding import PartitionSpec as P

LON = 1280


time_step = 0.8


def with_halo(value, sides, width):
    for axis, dim in sides:
        size, length = (lax.axis_size(axis), value.shape[dim])
        up = [(i, (i + 1) % size) for i in range(size - 1)]
        down = [(j, i) for i, j in up]
        last = lax.slice_in_dim(value, length - width, length, axis=dim)
        leading = lax.slice_in_dim(value, 0, width, axis=dim)
        before = lax.ppermute(last, axis, up)
        after = lax.ppermute(leading, axis, down)
        value = jnp.concatenate([before, value, after], axis=dim)
    return value


def damping(mode_depth, degree_of, degree_total):
    ratio = degree_of * (degree_of + 1.0) / float(degree_total * degree_total)
    return 1.0 / (1.0 + mode_depth[:, None] * ratio[None, :])


def trig_table(wave_map, lon_count):
    column = jnp.arange(lon_count, dtype=jnp.int32)
    product = wave_map[:, None] * column[None, :] % lon_count
    angles = product.astype(jnp.float32) * (2.0 * math.pi / lon_count)
    return jnp.stack([jnp.cos(angles), -jnp.sin(angles)], axis=1).astype(jnp.bfloat16)


def tendency(fields_ext):
    center = fields_ext[..., 1:-1, :]
    ahead_lon = jnp.roll(center, -1, axis=-1)
    behind_lon = jnp.roll(center, 1, axis=-1)
    ahead_lat = fields_ext[..., 2:, :]
    behind_lat = fields_ext[..., :-2, :]
    return center[0] * (ahead_lon - behind_lon) * 0.5 + center[1] * (ahead_lat - behind_lat) * 0.5


def legendre_rows(solved, legendre):
    band_rows = jnp.einsum(
        "lsfcn,snt->tlsfc", solved, legendre, preferred_element_type=jnp.float32
    ).astype(jnp.bfloat16)
    return band_rows.reshape(band_rows.shape[0], -1)


def general_path(spectral, modes_in, modes_out, mode_depth, legendre, wave_map, row_points):
    lev_rows = spectral.shape[0]
    wave_slots = spectral.shape[1]
    field_count = spectral.shape[2]
    degree_count = spectral.shape[4]
    shard_count = lax.axis_size("wave")
    first_slot = lax.axis_index("wave") * wave_slots
    local_waves = lax.dynamic_slice_in_dim(wave_map, first_slot, wave_slots)
    degrees = jnp.arange(degree_count, dtype=jnp.int32)
    keep_mask = degrees[None, :] >= local_waves[:, None]
    masked = jnp.where(keep_mask[None, :, None, None, :], spectral, jnp.zeros_like(spectral))
    flattened = masked.reshape(lev_rows, -1)
    trig_rows = trig_table(wave_map, LON).reshape(shard_count, wave_slots, 2, LON)
    norm_factor = 1.0 / math.sqrt(wave_map.shape[0])
    modal_part = jnp.dot(
        modes_in,
        lax.all_gather(flattened, "lev", axis=0, tiled=True),
        preferred_element_type=jnp.float32,
    )
    degree_of = (jnp.arange(flattened.shape[1], dtype=jnp.int32) % degree_count).astype(jnp.float32)
    scaled = (modal_part * damping(mode_depth, degree_of, degree_count)).astype(jnp.bfloat16)
    own_rows = lax.dynamic_slice_in_dim(modes_out, lax.axis_index("lev") * lev_rows, lev_rows, 0)
    solved = jnp.dot(own_rows, scaled, preferred_element_type=jnp.float32).astype(jnp.bfloat16)
    band_rows = legendre_rows(solved.reshape(spectral.shape), legendre)
    regrouped = lax.all_to_all(band_rows, "wave", split_axis=0, concat_axis=1, tiled=True)
    lat_rows = regrouped.shape[0]
    split_bands = regrouped.reshape(lat_rows, shard_count, lev_rows, wave_slots, field_count, 2)
    grid_field = (
        jnp.einsum("twlsfc,wscx->fltx", split_bands, trig_rows, preferred_element_type=jnp.float32)
        * norm_factor
    )
    wide_rows = with_halo(grid_field, (("wave", 2),), 2)
    section_wide = wide_rows[:, :, 1:-1, :] - time_step * tendency(wide_rows)
    second = 0.5 * (grid_field + section_wide[:, :, 1:-1, :] - time_step * tendency(section_wide))
    points = jnp.arange(LON, dtype=jnp.int32)[None, :] < row_points[:, None]
    return jnp.where(points[None, None, :, :], second, jnp.zeros_like(second))


def iota(shape, dim):
    return lax.broadcasted_iota(jnp.int32, shape, dim)


def trig_rows_of(waves, parts, points):
    rows = waves.shape[0]
    column = iota((rows, points), 1).astype(jnp.float32)
    product = waves * column + parts * (points / 4)
    turns = product * (1.0 / points)
    left = product - jnp.floor(turns) * points
    folded = 0.25 - jnp.abs(left * (1.0 / points) - 0.5)
    angle = folded * (2.0 * math.pi)
    square = angle * angle
    total = jnp.full_like(angle, -1.0 / math.factorial(11))
    for order in (9, 7, 5, 3, 1):
        sign = 1.0 if order % 4 == 1 else -1.0
        total = total * square + sign / math.factorial(order)
    return -(total * angle)


def exchange_kernel(
    dims, x_ref, min_hbm, mout_hbm, depth_hbm, leg_hbm, wm_hbm, points_hbm,
    bands_ref, table_ref, slope_ref, limit_ref,
    min_ref, mout_ref, depth_ref, leg_ref, wm_ref, points_ref,
    levels_buf, solved_buf, send_buf, recv_buf, wide,
    in_sem, own_sem, lev_send, lev_recv, all_send, all_recv,
):
    groups, shards, slots, lev_rows, fields, degrees, lat_total, scale = dims
    halo_rows = 8
    lat_rows = lat_total // shards
    part_slots = slots // groups
    everyone = groups * shards
    q = lax.axis_index("lev")
    w = lax.axis_index("wave")
    me = w * groups + q

    def coords(place):
        return (lax.rem(place, groups), lax.div(place, groups))

    barrier = pltpu.get_barrier_semaphore()

    def greet(step, carry):
        place = lax.rem(me + step, everyone)
        pl.semaphore_signal(barrier, inc=1, device_id=coords(place), device_id_type=pl.DeviceIdType.MESH)
        return carry

    lax.fori_loop(1, everyone, greet, 0)

    pairs = [
        (wm_hbm, wm_ref), (leg_hbm.at[pl.ds(q * part_slots, part_slots)], leg_ref),
        (depth_hbm, depth_ref), (points_hbm, points_ref), (min_hbm, min_ref), (mout_hbm, mout_ref),
    ]
    inputs = [pltpu.make_async_copy(a, b, in_sem.at[i]) for i, (a, b) in enumerate(pairs)]
    for copy in inputs:
        copy.start()
    own = pltpu.make_async_copy(x_ref.at[q], levels_buf.at[q], own_sem.at[0])
    own.start()

    pl.semaphore_wait(barrier, everyone - 1)

    def lev_copy(step):
        peer = lax.rem(q + step, groups)
        return pltpu.make_async_remote_copy(
            src_ref=x_ref.at[peer], dst_ref=levels_buf.at[q],
            send_sem=lev_send.at[peer], recv_sem=lev_recv.at[q],
            device_id=(peer, w), device_id_type=pl.DeviceIdType.MESH,
        )

    for step in range(1, groups):
        lev_copy(step).start()
    for copy in inputs:
        copy.wait()

    total_slots = shards * slots
    wm = wm_ref[...].astype(jnp.float32)
    pair = 2 * degrees
    halo_total = shards * halo_rows
    row = iota((halo_total, lat_total), 0)
    inner = row % halo_rows
    lat = (row // halo_rows) * lat_rows + jnp.where(inner < halo_rows - 2, inner, inner - halo_rows)
    pick = (lat == iota((halo_total, lat_total), 1)).astype(jnp.float32).astype(jnp.bfloat16)
    double = (iota((degrees, pair), 0) == iota((degrees, pair), 1) % degrees)
    double = double.astype(jnp.float32).astype(jnp.bfloat16)
    degree = (iota((halo_total, pair), 1) % degrees).astype(jnp.float32)
    legs = []
    for s in range(part_slots):
        leg = jnp.dot(leg_ref[s], double, preferred_element_type=jnp.float32)
        leg = jnp.dot(pick, leg.astype(jnp.bfloat16), preferred_element_type=jnp.float32)
        place = w * slots + q * part_slots + s
        chosen = iota((1, total_slots), 1) == place
        wave = jnp.sum(jnp.where(chosen, wm, 0.0), axis=1, keepdims=True)
        legs.append(jnp.where(degree >= wave, leg, 0.0).astype(jnp.bfloat16))
    legs = jnp.concatenate(legs, axis=1)
    modes = min_ref.shape[0]
    eye = iota((modes, modes), 0) == iota((modes, modes), 1)
    depth = jnp.sum(jnp.where(eye, depth_ref[...], 0.0), axis=1, keepdims=True)
    degree_row = (iota((modes, pair), 1) % degrees).astype(jnp.float32)
    ratio = degree_row * (degree_row + 1.0) / float(degrees * degrees)
    damp = 1.0 / (1.0 + depth * ratio)

    rows = 2 * total_slots
    row = iota((rows, total_slots), 0)
    slot = part_slots * (row % everyone) + row // (2 * everyone)
    waves = jnp.sum(jnp.where(slot == iota((rows, total_slots), 1), wm, 0.0), axis=1, keepdims=True)
    parts = ((iota((rows, 1), 0) // everyone) % 2).astype(jnp.float32)
    points = table_ref.shape[1]
    table = (trig_rows_of(waves, parts, points) * scale).astype(jnp.bfloat16)
    table_ref[...] = table
    table = table.astype(jnp.float32)
    slope = pltpu.roll(table, points - 1, 1) - pltpu.roll(table, 1, 1)
    high = slope.astype(jnp.bfloat16)
    slope_ref[:rows] = high
    slope_ref[rows:] = (slope - high.astype(jnp.float32)).astype(jnp.bfloat16)
    match = iota((limit_ref.shape[0], lat_rows), 0) == iota((limit_ref.shape[0], lat_rows), 1)
    limit = jnp.sum(jnp.where(match, points_ref[...].astype(jnp.float32), 0.0), axis=1, keepdims=True)
    limit_ref[...] = jnp.broadcast_to(limit, limit_ref.shape).astype(jnp.int32)

    own.wait()
    for step in range(1, groups):
        peer = lax.rem(q + step, groups)
        pltpu.make_async_remote_copy(
            src_ref=x_ref.at[peer], dst_ref=levels_buf.at[peer],
            send_sem=lev_send.at[peer], recv_sem=lev_recv.at[peer],
            device_id=(peer, w), device_id_type=pl.DeviceIdType.MESH,
        ).wait_recv()

    columns = levels_buf.shape[2]
    level_count = groups * lev_rows
    coef = levels_buf[...].reshape(level_count, columns)
    modal = jnp.dot(min_ref[...], coef, preferred_element_type=jnp.float32)
    scaled = jnp.concatenate(
        [modal[:, i * pair : (i + 1) * pair] * damp for i in range(columns // pair)], axis=1
    ).astype(jnp.bfloat16)
    solved = jnp.dot(mout_ref[...], scaled, preferred_element_type=jnp.float32).astype(jnp.bfloat16)
    solved_buf[...] = solved.reshape(groups, lev_rows, columns)

    def all_copy(peer, land):
        return pltpu.make_async_remote_copy(
            src_ref=send_buf.at[peer], dst_ref=recv_buf.at[land],
            send_sem=all_send.at[peer], recv_sem=all_recv.at[land],
            device_id=coords(peer), device_id_type=pl.DeviceIdType.MESH,
        )

    lane = iota((lev_rows, pair), 1)
    empty = jnp.zeros((2 * lev_rows, pair), jnp.bfloat16)
    for turn in range(groups):
        to = lax.rem(q + 1 + turn, groups)
        outs = []
        for f in range(fields):
            blocks = []
            for s in range(part_slots):
                at = (s * fields + f) * pair
                tile = solved_buf[to, :, at : at + pair]
                none = jnp.zeros_like(tile)
                split = [jnp.where(lane < degrees, tile, none), jnp.where(lane >= degrees, tile, none)]
                split = jnp.concatenate(split, axis=0)
                blocks.append(jnp.concatenate([split if k == s else empty for k in range(part_slots)], axis=1))
            outs.append(lax.dot_general(
                legs, jnp.concatenate(blocks, axis=0), (((1,), (1,)), ((), ())),
                preferred_element_type=jnp.float32,
            ))
        for shard in range(shards):
            at = shard * halo_rows
            message = jnp.concatenate([out[at : at + halo_rows] for out in outs], axis=0)
            send_buf[shard * groups + to] = message.astype(jnp.bfloat16)

        def start(step, carry):
            all_copy(lax.rem(w + step, shards) * groups + to, me).start()
            return carry

        lax.fori_loop(0 if turn < groups - 1 else 1, shards, start, 0)
    mine = pltpu.make_async_copy(send_buf.at[me], recv_buf.at[me], own_sem.at[1])
    mine.start()
    mine.wait()

    def finish(step, carry):
        peer = lax.rem(me + step, everyone)
        all_copy(peer, peer).wait_recv()
        return carry

    lax.fori_loop(1, everyone, finish, 0)
    message = fields * halo_rows
    wide[...] = recv_buf[...].reshape(everyone * message, rows).astype(jnp.float32)
    lane = iota((lev_rows, rows), 1) // everyone
    count = rows // everyone
    for first in range(0, message, count):
        stack = [wide[pl.ds(first + j, everyone, stride=message), :] for j in range(count)]
        turned = jnp.concatenate(stack, axis=0).T
        for j in range(count):
            value = None
            for g in range(count):
                part = turned[g * lev_rows : (g + 1) * lev_rows]
                if g != j:
                    part = pltpu.roll(part, ((g - j) * everyone) % rows, 1)
                value = part if value is None else jnp.where(lane == g, part, value)
            f, t = divmod(first + j, halo_rows)
            bands_ref[t, f] = value.astype(jnp.bfloat16)

    def sent(step, carry):
        all_copy(lax.rem(me + step, everyone), me).wait_send()
        return carry

    lax.fori_loop(1, everyone, sent, 0)
    for step in range(1, groups):
        lev_copy(step).wait_send()


def section_kernel(scale, limit_ref, bands_ref, table_ref, slope_ref, out_ref, grid_buf, lon_buf, first_buf):
    halo_rows, fields, chunk, depth = bands_ref.shape
    lat_rows, width = out_ref.shape[2], out_ref.shape[3]
    inner = [halo_rows - 1] + list(range(lat_rows + 1))

    def product(a, b):
        value = jnp.dot(a, b, preferred_element_type=jnp.float32)
        return (value if scale is None else value * scale).reshape(fields, chunk, width)

    for t in range(halo_rows):
        part = bands_ref[t].reshape(fields * chunk, depth)
        grid_buf[t] = product(part, table_ref[...])
        if t in inner:
            lon_buf[t] = product(jnp.concatenate([part, part], axis=1), slope_ref[...])

    def around(ref, t, f):
        return ref[(t + 1) % halo_rows, f] - ref[(t - 1) % halo_rows, f]

    for t in inner:
        east, north = grid_buf[t, 0] * (0.5 * time_step), grid_buf[t, 1] * (0.5 * time_step)
        for f in range(fields):
            first_buf[t, f] = grid_buf[t, f] - (east * lon_buf[t, f] + north * around(grid_buf, t, f))
    column = iota((chunk, width), 1)
    for t in range(lat_rows):
        east, north = first_buf[t, 0] * (0.25 * time_step), first_buf[t, 1] * (0.25 * time_step)
        keep = column < limit_ref[t : t + 1, :1]
        for f in range(fields):
            value = first_buf[t, f]
            lon = pltpu.roll(value, width - 1, 1) - pltpu.roll(value, 1, 1)
            second = 0.5 * (grid_buf[t, f] + value) - (east * lon + north * around(first_buf, t, f))
            out_ref[f, :, t, :] = jnp.where(keep, second, 0.0)


def per_device(spectral, modes_in, modes_out, mode_depth, legendre, wave_map, row_points):
    lev_rows, slots, fields, _, degrees = spectral.shape
    groups, shards = lax.axis_size("lev"), lax.axis_size("wave")
    lat_total = legendre.shape[2]
    lat_rows = lat_total // shards
    everyone, halo_rows = groups * shards, 8
    part_slots = slots // groups
    rows = 2 * shards * slots
    fits = slots == 2 * groups and 2 * degrees == 128 and lat_rows == 4
    fits = fits and lev_rows == 32 and everyone == 32 and rows == 128
    if not fits:
        return general_path(spectral, modes_in, modes_out, mode_depth, legendre, wave_map, row_points)
    norm = 1.0 / math.sqrt(shards * slots)
    exact = math.frexp(norm)[0] == 0.5
    columns = part_slots * fields * 2 * degrees
    modes = modes_in.shape[0]
    x = spectral.reshape(lev_rows, groups, columns).transpose(1, 0, 2)
    dims = (groups, shards, slots, lev_rows, fields, degrees, lat_total, norm if exact else 1.0)
    vmem = pl.BlockSpec(memory_space=pltpu.VMEM)
    hbm = pl.BlockSpec(memory_space=pltpu.HBM)
    message = fields * halo_rows
    bf16 = jnp.bfloat16
    bands, table, slope, limit = pl.pallas_call(
        functools.partial(exchange_kernel, dims),
        out_shape=(
            jax.ShapeDtypeStruct((halo_rows, fields, lev_rows, rows), bf16),
            jax.ShapeDtypeStruct((rows, LON), bf16),
            jax.ShapeDtypeStruct((2 * rows, LON), bf16),
            jax.ShapeDtypeStruct((8, 128), jnp.int32),
        ),
        in_specs=[vmem] + [hbm] * 6,
        out_specs=(vmem,) * 4,
        scratch_shapes=[
            pltpu.VMEM((modes, modes), bf16),
            pltpu.VMEM((modes, modes), bf16),
            pltpu.VMEM((1, modes), jnp.float32),
            pltpu.VMEM((part_slots, lat_total, degrees), bf16),
            pltpu.VMEM((1, shards * slots), jnp.int32),
            pltpu.VMEM((1, lat_rows), jnp.int32),
            pltpu.VMEM((groups, lev_rows, columns), bf16),
            pltpu.VMEM((groups, lev_rows, columns), bf16),
            pltpu.VMEM((everyone, message, rows), bf16),
            pltpu.VMEM((everyone, message, rows), bf16),
            pltpu.VMEM((everyone * message, rows), jnp.float32),
            pltpu.SemaphoreType.DMA((6,)),
            pltpu.SemaphoreType.DMA((2,)),
            pltpu.SemaphoreType.DMA((groups,)),
            pltpu.SemaphoreType.DMA((groups,)),
            pltpu.SemaphoreType.DMA((everyone,)),
            pltpu.SemaphoreType.DMA((everyone,)),
        ],
        compiler_params=pltpu.CompilerParams(
            collective_id=0, has_side_effects=True, vmem_limit_bytes=32 * 1024 * 1024
        ),
        name="exchange",
    )(
        x, modes_in, modes_out, mode_depth.reshape(1, -1), jnp.swapaxes(legendre, 1, 2),
        wave_map.reshape(1, -1), row_points.reshape(1, -1),
    )
    chunk = 16
    return pl.pallas_call(
        functools.partial(section_kernel, None if exact else norm),
        grid=(lev_rows // chunk,),
        out_shape=jax.ShapeDtypeStruct((fields, lev_rows, lat_rows, LON), jnp.float32),
        in_specs=[
            pl.BlockSpec((8, 128), lambda i: (0, 0)),
            pl.BlockSpec((halo_rows, fields, chunk, rows), lambda i: (0, 0, i, 0)),
            pl.BlockSpec((rows, LON), lambda i: (0, 0)),
            pl.BlockSpec((2 * rows, LON), lambda i: (0, 0)),
        ],
        out_specs=pl.BlockSpec((fields, chunk, lat_rows, LON), lambda i: (0, i, 0, 0)),
        scratch_shapes=[pltpu.VMEM((halo_rows, fields, chunk, LON), jnp.float32)] * 3,
        compiler_params=pltpu.CompilerParams(vmem_limit_bytes=48 * 1024 * 1024),
        name="sections",
    )(limit, bands, table, slope)


def solution(mesh):
    in_specs = (
        P("lev", "wave", None, None, None),
        P(),
        P(),
        P(),
        P("wave", None, None),
        P(),
        P("wave"),
    )
    out_specs = P(None, "lev", "wave", None)
    return jax.shard_map(
        per_device, mesh=mesh, in_specs=in_specs, out_specs=out_specs, check_vma=False
    )
```

```python
import functools
import math

import jax
import jax.numpy as jnp
from jax import lax
from jax.experimental import pallas as pl
from jax.experimental.pallas import tpu as pltpu
from jax.sharding import PartitionSpec as P

LON = 1280


time_step = 0.8


def with_halo(value, sides, width):
    for axis, dim in sides:
        size, length = (lax.axis_size(axis), value.shape[dim])
        up = [(i, (i + 1) % size) for i in range(size - 1)]
        down = [(j, i) for i, j in up]
        last = lax.slice_in_dim(value, length - width, length, axis=dim)
        leading = lax.slice_in_dim(value, 0, width, axis=dim)
        before = lax.ppermute(last, axis, up)
        after = lax.ppermute(leading, axis, down)
        value = jnp.concatenate([before, value, after], axis=dim)
    return value


def damping(mode_depth, degree_of, degree_total):
    ratio = degree_of * (degree_of + 1.0) / float(degree_total * degree_total)
    return 1.0 / (1.0 + mode_depth[:, None] * ratio[None, :])


def trig_table(wave_map, lon_count):
    column = jnp.arange(lon_count, dtype=jnp.int32)
    product = wave_map[:, None] * column[None, :] % lon_count
    angles = product.astype(jnp.float32) * (2.0 * math.pi / lon_count)
    return jnp.stack([jnp.cos(angles), -jnp.sin(angles)], axis=1).astype(jnp.bfloat16)


def tendency(fields_ext):
    center = fields_ext[..., 1:-1, :]
    ahead_lon = jnp.roll(center, -1, axis=-1)
    behind_lon = jnp.roll(center, 1, axis=-1)
    ahead_lat = fields_ext[..., 2:, :]
    behind_lat = fields_ext[..., :-2, :]
    return center[0] * (ahead_lon - behind_lon) * 0.5 + center[1] * (ahead_lat - behind_lat) * 0.5


def legendre_rows(solved, legendre):
    band_rows = jnp.einsum(
        "lsfcn,snt->tlsfc", solved, legendre, preferred_element_type=jnp.float32
    ).astype(jnp.bfloat16)
    return band_rows.reshape(band_rows.shape[0], -1)


def general_path(spectral, modes_in, modes_out, mode_depth, legendre, wave_map, row_points):
    lev_rows = spectral.shape[0]
    wave_slots = spectral.shape[1]
    field_count = spectral.shape[2]
    degree_count = spectral.shape[4]
    shard_count = lax.axis_size("wave")
    first_slot = lax.axis_index("wave") * wave_slots
    local_waves = lax.dynamic_slice_in_dim(wave_map, first_slot, wave_slots)
    degrees = jnp.arange(degree_count, dtype=jnp.int32)
    keep_mask = degrees[None, :] >= local_waves[:, None]
    masked = jnp.where(keep_mask[None, :, None, None, :], spectral, jnp.zeros_like(spectral))
    flattened = masked.reshape(lev_rows, -1)
    trig_rows = trig_table(wave_map, LON).reshape(shard_count, wave_slots, 2, LON)
    norm_factor = 1.0 / math.sqrt(wave_map.shape[0])
    modal_part = jnp.dot(
        modes_in,
        lax.all_gather(flattened, "lev", axis=0, tiled=True),
        preferred_element_type=jnp.float32,
    )
    degree_of = (jnp.arange(flattened.shape[1], dtype=jnp.int32) % degree_count).astype(jnp.float32)
    scaled = (modal_part * damping(mode_depth, degree_of, degree_count)).astype(jnp.bfloat16)
    own_rows = lax.dynamic_slice_in_dim(modes_out, lax.axis_index("lev") * lev_rows, lev_rows, 0)
    solved = jnp.dot(own_rows, scaled, preferred_element_type=jnp.float32).astype(jnp.bfloat16)
    band_rows = legendre_rows(solved.reshape(spectral.shape), legendre)
    regrouped = lax.all_to_all(band_rows, "wave", split_axis=0, concat_axis=1, tiled=True)
    lat_rows = regrouped.shape[0]
    split_bands = regrouped.reshape(lat_rows, shard_count, lev_rows, wave_slots, field_count, 2)
    grid_field = (
        jnp.einsum("twlsfc,wscx->fltx", split_bands, trig_rows, preferred_element_type=jnp.float32)
        * norm_factor
    )
    wide_rows = with_halo(grid_field, (("wave", 2),), 2)
    section_wide = wide_rows[:, :, 1:-1, :] - time_step * tendency(wide_rows)
    second = 0.5 * (grid_field + section_wide[:, :, 1:-1, :] - time_step * tendency(section_wide))
    points = jnp.arange(LON, dtype=jnp.int32)[None, :] < row_points[:, None]
    return jnp.where(points[None, None, :, :], second, jnp.zeros_like(second))


def iota(shape, dim):
    return lax.broadcasted_iota(jnp.int32, shape, dim)


def trig_rows_of(waves, parts, points):
    rows = waves.shape[0]
    column = iota((rows, points), 1).astype(jnp.float32)
    product = waves * column + parts * (points / 4)
    turns = product * (1.0 / points)
    left = product - jnp.floor(turns) * points
    folded = 0.25 - jnp.abs(left * (1.0 / points) - 0.5)
    angle = folded * (2.0 * math.pi)
    square = angle * angle
    total = jnp.full_like(angle, -1.0 / math.factorial(11))
    for order in (9, 7, 5, 3, 1):
        sign = 1.0 if order % 4 == 1 else -1.0
        total = total * square + sign / math.factorial(order)
    return -(total * angle)


def exchange_kernel(
    dims, x_ref, min_hbm, mout_hbm, depth_hbm, leg_hbm, wm_hbm, points_hbm,
    bands_ref, table_hbm, slope_hbm, limit_hbm,
    table_ref, slope_ref, limit_ref, min_ref, mout_ref, depth_ref, leg_ref, wm_ref, points_ref,
    levels_buf, solved_buf, send_buf, recv_buf, wide,
    in_sem, out_sem, own_sem, lev_send, lev_recv, all_send, all_recv,
):
    groups, shards, slots, lev_rows, fields, degrees, lat_total, scale = dims
    halo_rows = 8
    lat_rows = lat_total // shards
    part_slots = slots // groups
    everyone = groups * shards
    q = lax.axis_index("lev")
    w = lax.axis_index("wave")
    me = w * groups + q

    def coords(place):
        return (lax.rem(place, groups), lax.div(place, groups))

    barrier = pltpu.get_barrier_semaphore()

    def greet(step, carry):
        place = lax.rem(me + step, everyone)
        pl.semaphore_signal(barrier, inc=1, device_id=coords(place), device_id_type=pl.DeviceIdType.MESH)
        return carry

    lax.fori_loop(1, everyone, greet, 0)

    pairs = [
        (wm_hbm, wm_ref), (leg_hbm.at[pl.ds(q * part_slots, part_slots)], leg_ref),
        (depth_hbm, depth_ref), (points_hbm, points_ref), (min_hbm, min_ref), (mout_hbm, mout_ref),
    ]
    inputs = [pltpu.make_async_copy(a, b, in_sem.at[i]) for i, (a, b) in enumerate(pairs)]
    for copy in inputs:
        copy.start()
    own = pltpu.make_async_copy(x_ref.at[q], levels_buf.at[q], own_sem.at[0])
    own.start()

    pl.semaphore_wait(barrier, everyone - 1)

    def lev_copy(step):
        peer = lax.rem(q + step, groups)
        return pltpu.make_async_remote_copy(
            src_ref=x_ref.at[peer], dst_ref=levels_buf.at[q],
            send_sem=lev_send.at[peer], recv_sem=lev_recv.at[q],
            device_id=(peer, w), device_id_type=pl.DeviceIdType.MESH,
        )

    for step in range(1, groups):
        lev_copy(step).start()
    for copy in inputs:
        copy.wait()

    total_slots = shards * slots
    wm = wm_ref[...].astype(jnp.float32)
    pair = 2 * degrees
    halo_total = shards * halo_rows
    row = iota((halo_total, lat_total), 0)
    inner = row % halo_rows
    lat = (row // halo_rows) * lat_rows + jnp.where(inner < halo_rows - 2, inner, inner - halo_rows)
    pick = (lat == iota((halo_total, lat_total), 1)).astype(jnp.float32).astype(jnp.bfloat16)
    double = (iota((degrees, pair), 0) == iota((degrees, pair), 1) % degrees)
    double = double.astype(jnp.float32).astype(jnp.bfloat16)
    degree = (iota((halo_total, pair), 1) % degrees).astype(jnp.float32)
    legs = []
    for s in range(part_slots):
        leg = jnp.dot(leg_ref[s], double, preferred_element_type=jnp.float32)
        leg = jnp.dot(pick, leg.astype(jnp.bfloat16), preferred_element_type=jnp.float32)
        place = w * slots + q * part_slots + s
        chosen = iota((1, total_slots), 1) == place
        wave = jnp.sum(jnp.where(chosen, wm, 0.0), axis=1, keepdims=True)
        legs.append(jnp.where(degree >= wave, leg, 0.0).astype(jnp.bfloat16))
    legs = jnp.concatenate(legs, axis=1)
    modes = min_ref.shape[0]
    eye = iota((modes, modes), 0) == iota((modes, modes), 1)
    depth = jnp.sum(jnp.where(eye, depth_ref[...], 0.0), axis=1, keepdims=True)
    degree_row = (iota((modes, pair), 1) % degrees).astype(jnp.float32)
    ratio = degree_row * (degree_row + 1.0) / float(degrees * degrees)
    damp = 1.0 / (1.0 + depth * ratio)

    rows = 2 * total_slots
    row = iota((rows, total_slots), 0)
    slot = part_slots * (row % everyone) + row // (2 * everyone)
    waves = jnp.sum(jnp.where(slot == iota((rows, total_slots), 1), wm, 0.0), axis=1, keepdims=True)
    parts = ((iota((rows, 1), 0) // everyone) % 2).astype(jnp.float32)
    points = table_ref.shape[1]
    table = (trig_rows_of(waves, parts, points) * scale).astype(jnp.bfloat16)
    table_ref[...] = table
    table = table.astype(jnp.float32)
    slope = pltpu.roll(table, points - 1, 1) - pltpu.roll(table, 1, 1)
    high = slope.astype(jnp.bfloat16)
    slope_ref[:rows] = high
    slope_ref[rows:] = (slope - high.astype(jnp.float32)).astype(jnp.bfloat16)
    match = iota((limit_ref.shape[0], lat_rows), 0) == iota((limit_ref.shape[0], lat_rows), 1)
    limit = jnp.sum(jnp.where(match, points_ref[...].astype(jnp.float32), 0.0), axis=1, keepdims=True)
    limit_ref[...] = jnp.broadcast_to(limit, limit_ref.shape).astype(jnp.int32)
    pairs = [(table_ref, table_hbm), (slope_ref, slope_hbm), (limit_ref, limit_hbm)]
    outputs = [pltpu.make_async_copy(a, b, out_sem.at[i]) for i, (a, b) in enumerate(pairs)]
    for copy in outputs:
        copy.start()

    own.wait()
    for step in range(1, groups):
        peer = lax.rem(q + step, groups)
        pltpu.make_async_remote_copy(
            src_ref=x_ref.at[peer], dst_ref=levels_buf.at[peer],
            send_sem=lev_send.at[peer], recv_sem=lev_recv.at[peer],
            device_id=(peer, w), device_id_type=pl.DeviceIdType.MESH,
        ).wait_recv()

    columns = levels_buf.shape[2]
    level_count = groups * lev_rows
    coef = levels_buf[...].reshape(level_count, columns)
    modal = jnp.dot(min_ref[...], coef, preferred_element_type=jnp.float32)
    scaled = jnp.concatenate(
        [modal[:, i * pair : (i + 1) * pair] * damp for i in range(columns // pair)], axis=1
    ).astype(jnp.bfloat16)
    solved = jnp.dot(mout_ref[...], scaled, preferred_element_type=jnp.float32).astype(jnp.bfloat16)
    solved_buf[...] = solved.reshape(groups, lev_rows, columns)

    def all_copy(peer, land):
        return pltpu.make_async_remote_copy(
            src_ref=send_buf.at[peer], dst_ref=recv_buf.at[land],
            send_sem=all_send.at[peer], recv_sem=all_recv.at[land],
            device_id=coords(peer), device_id_type=pl.DeviceIdType.MESH,
        )

    lane = iota((lev_rows, pair), 1)
    empty = jnp.zeros((2 * lev_rows, pair), jnp.bfloat16)
    for turn in range(groups):
        to = lax.rem(q + 1 + turn, groups)
        outs = []
        for f in range(fields):
            blocks = []
            for s in range(part_slots):
                at = (s * fields + f) * pair
                tile = solved_buf[to, :, at : at + pair]
                none = jnp.zeros_like(tile)
                split = [jnp.where(lane < degrees, tile, none), jnp.where(lane >= degrees, tile, none)]
                split = jnp.concatenate(split, axis=0)
                blocks.append(jnp.concatenate([split if k == s else empty for k in range(part_slots)], axis=1))
            outs.append(lax.dot_general(
                legs, jnp.concatenate(blocks, axis=0), (((1,), (1,)), ((), ())),
                preferred_element_type=jnp.float32,
            ))
        for shard in range(shards):
            at = shard * halo_rows
            message = jnp.concatenate([out[at : at + halo_rows] for out in outs], axis=0)
            send_buf[shard * groups + to] = message.astype(jnp.bfloat16)

        def start(step, carry):
            all_copy(lax.rem(w + step, shards) * groups + to, me).start()
            return carry

        lax.fori_loop(0 if turn < groups - 1 else 1, shards, start, 0)
    mine = pltpu.make_async_copy(send_buf.at[me], recv_buf.at[me], own_sem.at[1])
    mine.start()
    mine.wait()

    def finish(step, carry):
        peer = lax.rem(me + step, everyone)
        all_copy(peer, peer).wait_recv()
        return carry

    lax.fori_loop(1, everyone, finish, 0)
    message = fields * halo_rows
    wide[...] = recv_buf[...].reshape(everyone * message, rows).astype(jnp.float32)
    lane = iota((lev_rows, rows), 1) // everyone
    count = rows // everyone
    for first in range(0, message, count):
        stack = [wide[pl.ds(first + j, everyone, stride=message), :] for j in range(count)]
        turned = jnp.concatenate(stack, axis=0).T
        for j in range(count):
            value = None
            for g in range(count):
                part = turned[g * lev_rows : (g + 1) * lev_rows]
                if g != j:
                    part = pltpu.roll(part, ((g - j) * everyone) % rows, 1)
                value = part if value is None else jnp.where(lane == g, part, value)
            f, t = divmod(first + j, halo_rows)
            bands_ref[t, f] = value.astype(jnp.bfloat16)

    def sent(step, carry):
        all_copy(lax.rem(me + step, everyone), me).wait_send()
        return carry

    lax.fori_loop(1, everyone, sent, 0)
    for step in range(1, groups):
        lev_copy(step).wait_send()
    for copy in outputs:
        copy.wait()


def section_kernel(scale, limit_ref, bands_ref, table_ref, slope_ref, out_ref, grid_buf, lon_buf, first_buf):
    halo_rows, fields, chunk, depth = bands_ref.shape
    lat_rows, width = out_ref.shape[2], out_ref.shape[3]
    inner = [halo_rows - 1] + list(range(lat_rows + 1))

    def product(a, b):
        value = jnp.dot(a, b, preferred_element_type=jnp.float32)
        return (value if scale is None else value * scale).reshape(fields, chunk, width)

    for t in range(halo_rows):
        part = bands_ref[t].reshape(fields * chunk, depth)
        grid_buf[t] = product(part, table_ref[...])
        if t in inner:
            lon_buf[t] = product(jnp.concatenate([part, part], axis=1), slope_ref[...])

    def around(ref, t, f):
        return ref[(t + 1) % halo_rows, f] - ref[(t - 1) % halo_rows, f]

    for t in inner:
        east, north = grid_buf[t, 0] * (0.5 * time_step), grid_buf[t, 1] * (0.5 * time_step)
        for f in range(fields):
            first_buf[t, f] = grid_buf[t, f] - (east * lon_buf[t, f] + north * around(grid_buf, t, f))
    column = iota((chunk, width), 1)
    for t in range(lat_rows):
        east, north = first_buf[t, 0] * (0.25 * time_step), first_buf[t, 1] * (0.25 * time_step)
        keep = column < limit_ref[t : t + 1, :1]
        for f in range(fields):
            value = first_buf[t, f]
            lon = pltpu.roll(value, width - 1, 1) - pltpu.roll(value, 1, 1)
            second = 0.5 * (grid_buf[t, f] + value) - (east * lon + north * around(first_buf, t, f))
            out_ref[f, :, t, :] = jnp.where(keep, second, 0.0)


def per_device(spectral, modes_in, modes_out, mode_depth, legendre, wave_map, row_points):
    lev_rows, slots, fields, _, degrees = spectral.shape
    groups, shards = lax.axis_size("lev"), lax.axis_size("wave")
    lat_total = legendre.shape[2]
    lat_rows = lat_total // shards
    everyone, halo_rows = groups * shards, 8
    part_slots = slots // groups
    rows = 2 * shards * slots
    fits = slots == 2 * groups and 2 * degrees == 128 and lat_rows == 4
    fits = fits and lev_rows == 32 and everyone == 32 and rows == 128
    if not fits:
        return general_path(spectral, modes_in, modes_out, mode_depth, legendre, wave_map, row_points)
    norm = 1.0 / math.sqrt(shards * slots)
    exact = math.frexp(norm)[0] == 0.5
    columns = part_slots * fields * 2 * degrees
    modes = modes_in.shape[0]
    x = spectral.reshape(lev_rows, groups, columns).transpose(1, 0, 2)
    dims = (groups, shards, slots, lev_rows, fields, degrees, lat_total, norm if exact else 1.0)
    vmem = pl.BlockSpec(memory_space=pltpu.VMEM)
    hbm = pl.BlockSpec(memory_space=pltpu.HBM)
    message = fields * halo_rows
    bf16 = jnp.bfloat16
    bands, table, slope, limit = pl.pallas_call(
        functools.partial(exchange_kernel, dims),
        out_shape=(
            jax.ShapeDtypeStruct((halo_rows, fields, lev_rows, rows), bf16),
            jax.ShapeDtypeStruct((rows, LON), bf16),
            jax.ShapeDtypeStruct((2 * rows, LON), bf16),
            jax.ShapeDtypeStruct((8, 128), jnp.int32),
        ),
        in_specs=[hbm] * 7,
        out_specs=(vmem, hbm, hbm, hbm),
        scratch_shapes=[
            pltpu.VMEM((rows, LON), bf16),
            pltpu.VMEM((2 * rows, LON), bf16),
            pltpu.VMEM((8, 128), jnp.int32),
            pltpu.VMEM((modes, modes), bf16),
            pltpu.VMEM((modes, modes), bf16),
            pltpu.VMEM((1, modes), jnp.float32),
            pltpu.VMEM((part_slots, lat_total, degrees), bf16),
            pltpu.VMEM((1, shards * slots), jnp.int32),
            pltpu.VMEM((1, lat_rows), jnp.int32),
            pltpu.VMEM((groups, lev_rows, columns), bf16),
            pltpu.VMEM((groups, lev_rows, columns), bf16),
            pltpu.VMEM((everyone, message, rows), bf16),
            pltpu.VMEM((everyone, message, rows), bf16),
            pltpu.VMEM((everyone * message, rows), jnp.float32),
            pltpu.SemaphoreType.DMA((6,)),
            pltpu.SemaphoreType.DMA((3,)),
            pltpu.SemaphoreType.DMA((2,)),
            pltpu.SemaphoreType.DMA((groups,)),
            pltpu.SemaphoreType.DMA((groups,)),
            pltpu.SemaphoreType.DMA((everyone,)),
            pltpu.SemaphoreType.DMA((everyone,)),
        ],
        compiler_params=pltpu.CompilerParams(
            collective_id=0, has_side_effects=True, vmem_limit_bytes=60 * 1024 * 1024
        ),
        name="exchange",
    )(
        x, modes_in, modes_out, mode_depth.reshape(1, -1), jnp.swapaxes(legendre, 1, 2),
        wave_map.reshape(1, -1), row_points.reshape(1, -1),
    )
    chunk = 16
    return pl.pallas_call(
        functools.partial(section_kernel, None if exact else norm),
        grid=(lev_rows // chunk,),
        out_shape=jax.ShapeDtypeStruct((fields, lev_rows, lat_rows, LON), jnp.float32),
        in_specs=[
            pl.BlockSpec((8, 128), lambda i: (0, 0)),
            pl.BlockSpec((halo_rows, fields, chunk, rows), lambda i: (0, 0, i, 0)),
            pl.BlockSpec((rows, LON), lambda i: (0, 0)),
            pl.BlockSpec((2 * rows, LON), lambda i: (0, 0)),
        ],
        out_specs=pl.BlockSpec((fields, chunk, lat_rows, LON), lambda i: (0, i, 0, 0)),
        scratch_shapes=[pltpu.VMEM((halo_rows, fields, chunk, LON), jnp.float32)] * 3,
        compiler_params=pltpu.CompilerParams(vmem_limit_bytes=60 * 1024 * 1024),
        name="sections",
    )(limit, bands, table, slope)


def solution(mesh):
    in_specs = (
        P("lev", "wave", None, None, None),
        P(),
        P(),
        P(),
        P("wave", None, None),
        P(),
        P("wave"),
    )
    out_specs = P(None, "lev", "wave", None)
    return jax.shard_map(
        per_device, mesh=mesh, in_specs=in_specs, out_specs=out_specs, check_vma=False
    )
```

```python
import functools
import math

import jax
import jax.numpy as jnp
from jax import lax
from jax.experimental import pallas as pl
from jax.experimental.pallas import tpu as pltpu
from jax.sharding import PartitionSpec as P

LON = 1280


time_step = 0.8


def with_halo(value, sides, width):
    for axis, dim in sides:
        size, length = (lax.axis_size(axis), value.shape[dim])
        up = [(i, (i + 1) % size) for i in range(size - 1)]
        down = [(j, i) for i, j in up]
        last = lax.slice_in_dim(value, length - width, length, axis=dim)
        leading = lax.slice_in_dim(value, 0, width, axis=dim)
        before = lax.ppermute(last, axis, up)
        after = lax.ppermute(leading, axis, down)
        value = jnp.concatenate([before, value, after], axis=dim)
    return value


def damping(mode_depth, degree_of, degree_total):
    ratio = degree_of * (degree_of + 1.0) / float(degree_total * degree_total)
    return 1.0 / (1.0 + mode_depth[:, None] * ratio[None, :])


def trig_table(wave_map, lon_count):
    column = jnp.arange(lon_count, dtype=jnp.int32)
    product = wave_map[:, None] * column[None, :] % lon_count
    angles = product.astype(jnp.float32) * (2.0 * math.pi / lon_count)
    return jnp.stack([jnp.cos(angles), -jnp.sin(angles)], axis=1).astype(jnp.bfloat16)


def tendency(fields_ext):
    center = fields_ext[..., 1:-1, :]
    ahead_lon = jnp.roll(center, -1, axis=-1)
    behind_lon = jnp.roll(center, 1, axis=-1)
    ahead_lat = fields_ext[..., 2:, :]
    behind_lat = fields_ext[..., :-2, :]
    return center[0] * (ahead_lon - behind_lon) * 0.5 + center[1] * (ahead_lat - behind_lat) * 0.5


def legendre_rows(solved, legendre):
    band_rows = jnp.einsum(
        "lsfcn,snt->tlsfc", solved, legendre, preferred_element_type=jnp.float32
    ).astype(jnp.bfloat16)
    return band_rows.reshape(band_rows.shape[0], -1)


def general_path(spectral, modes_in, modes_out, mode_depth, legendre, wave_map, row_points):
    lev_rows = spectral.shape[0]
    wave_slots = spectral.shape[1]
    field_count = spectral.shape[2]
    degree_count = spectral.shape[4]
    shard_count = lax.axis_size("wave")
    first_slot = lax.axis_index("wave") * wave_slots
    local_waves = lax.dynamic_slice_in_dim(wave_map, first_slot, wave_slots)
    degrees = jnp.arange(degree_count, dtype=jnp.int32)
    keep_mask = degrees[None, :] >= local_waves[:, None]
    masked = jnp.where(keep_mask[None, :, None, None, :], spectral, jnp.zeros_like(spectral))
    flattened = masked.reshape(lev_rows, -1)
    trig_rows = trig_table(wave_map, LON).reshape(shard_count, wave_slots, 2, LON)
    norm_factor = 1.0 / math.sqrt(wave_map.shape[0])
    modal_part = jnp.dot(
        modes_in,
        lax.all_gather(flattened, "lev", axis=0, tiled=True),
        preferred_element_type=jnp.float32,
    )
    degree_of = (jnp.arange(flattened.shape[1], dtype=jnp.int32) % degree_count).astype(jnp.float32)
    scaled = (modal_part * damping(mode_depth, degree_of, degree_count)).astype(jnp.bfloat16)
    own_rows = lax.dynamic_slice_in_dim(modes_out, lax.axis_index("lev") * lev_rows, lev_rows, 0)
    solved = jnp.dot(own_rows, scaled, preferred_element_type=jnp.float32).astype(jnp.bfloat16)
    band_rows = legendre_rows(solved.reshape(spectral.shape), legendre)
    regrouped = lax.all_to_all(band_rows, "wave", split_axis=0, concat_axis=1, tiled=True)
    lat_rows = regrouped.shape[0]
    split_bands = regrouped.reshape(lat_rows, shard_count, lev_rows, wave_slots, field_count, 2)
    grid_field = (
        jnp.einsum("twlsfc,wscx->fltx", split_bands, trig_rows, preferred_element_type=jnp.float32)
        * norm_factor
    )
    wide_rows = with_halo(grid_field, (("wave", 2),), 2)
    section_wide = wide_rows[:, :, 1:-1, :] - time_step * tendency(wide_rows)
    second = 0.5 * (grid_field + section_wide[:, :, 1:-1, :] - time_step * tendency(section_wide))
    points = jnp.arange(LON, dtype=jnp.int32)[None, :] < row_points[:, None]
    return jnp.where(points[None, None, :, :], second, jnp.zeros_like(second))


def iota(shape, dim):
    return lax.broadcasted_iota(jnp.int32, shape, dim)


def trig_rows_of(waves, parts, points):
    rows = waves.shape[0]
    column = iota((rows, points), 1).astype(jnp.float32)
    product = waves * column + parts * (points / 4)
    turns = product * (1.0 / points)
    left = product - jnp.floor(turns) * points
    folded = 0.25 - jnp.abs(left * (1.0 / points) - 0.5)
    angle = folded * (2.0 * math.pi)
    square = angle * angle
    total = jnp.full_like(angle, -1.0 / math.factorial(11))
    for order in (9, 7, 5, 3, 1):
        sign = 1.0 if order % 4 == 1 else -1.0
        total = total * square + sign / math.factorial(order)
    return -(total * angle)


def exchange_kernel(
    dims, x_ref, min_hbm, mout_hbm, depth_hbm, leg_hbm, wm_hbm, points_hbm,
    bands_ref, table_hbm, slope_hbm, limit_hbm,
    table_ref, slope_ref, limit_ref, min_ref, mout_ref, depth_ref, leg_ref, wm_ref, points_ref,
    levels_buf, solved_buf, send_buf, recv_buf, wide,
    in_sem, out_sem, own_sem, lev_send, lev_recv, all_send, all_recv,
):
    groups, shards, slots, lev_rows, fields, degrees, lat_total, scale = dims
    halo_rows = 8
    lat_rows = lat_total // shards
    part_slots = slots // groups
    everyone = groups * shards
    q = lax.axis_index("lev")
    w = lax.axis_index("wave")
    me = w * groups + q

    def coords(place):
        return (lax.rem(place, groups), lax.div(place, groups))

    barrier = pltpu.get_barrier_semaphore()

    def greet(step, carry):
        place = lax.rem(me + step, everyone)
        pl.semaphore_signal(barrier, inc=1, device_id=coords(place), device_id_type=pl.DeviceIdType.MESH)
        return carry

    lax.fori_loop(1, everyone, greet, 0)

    pairs = [
        (wm_hbm, wm_ref), (leg_hbm.at[pl.ds(q * part_slots, part_slots)], leg_ref),
        (depth_hbm, depth_ref), (points_hbm, points_ref), (min_hbm, min_ref), (mout_hbm, mout_ref),
    ]
    inputs = [pltpu.make_async_copy(a, b, in_sem.at[i]) for i, (a, b) in enumerate(pairs)]
    for copy in inputs:
        copy.start()
    columns = levels_buf.shape[2]

    def part_of(peer):
        return x_ref.at[:, pl.ds(pl.multiple_of(peer * columns, 128), columns)]

    own = pltpu.make_async_copy(part_of(q), levels_buf.at[q], own_sem.at[0])
    own.start()

    for copy in inputs:
        copy.wait()

    total_slots = shards * slots
    wm = wm_ref[...].astype(jnp.float32)
    pair = 2 * degrees
    halo_total = shards * halo_rows
    row = iota((halo_total, lat_total), 0)
    inner = row % halo_rows
    lat = (row // halo_rows) * lat_rows + jnp.where(inner < halo_rows - 2, inner, inner - halo_rows)
    pick = (lat == iota((halo_total, lat_total), 1)).astype(jnp.float32).astype(jnp.bfloat16)
    double = (iota((degrees, pair), 0) == iota((degrees, pair), 1) % degrees)
    double = double.astype(jnp.float32).astype(jnp.bfloat16)
    degree = (iota((halo_total, pair), 1) % degrees).astype(jnp.float32)
    legs = []
    for s in range(part_slots):
        leg = jnp.dot(leg_ref[s], double, preferred_element_type=jnp.float32)
        leg = jnp.dot(pick, leg.astype(jnp.bfloat16), preferred_element_type=jnp.float32)
        place = w * slots + q * part_slots + s
        chosen = iota((1, total_slots), 1) == place
        wave = jnp.sum(jnp.where(chosen, wm, 0.0), axis=1, keepdims=True)
        legs.append(jnp.where(degree >= wave, leg, 0.0).astype(jnp.bfloat16))
    legs = jnp.concatenate(legs, axis=1)
    modes = min_ref.shape[0]
    eye = iota((modes, modes), 0) == iota((modes, modes), 1)
    depth = jnp.sum(jnp.where(eye, depth_ref[...], 0.0), axis=1, keepdims=True)
    degree_row = (iota((modes, pair), 1) % degrees).astype(jnp.float32)
    ratio = degree_row * (degree_row + 1.0) / float(degrees * degrees)
    damp = 1.0 / (1.0 + depth * ratio)

    pl.semaphore_wait(barrier, everyone - 1)

    def lev_copy(step):
        peer = lax.rem(q + step, groups)
        return pltpu.make_async_remote_copy(
            src_ref=part_of(peer), dst_ref=levels_buf.at[q],
            send_sem=lev_send.at[peer], recv_sem=lev_recv.at[q],
            device_id=(peer, w), device_id_type=pl.DeviceIdType.MESH,
        )

    for step in range(1, groups):
        lev_copy(step).start()
    own.wait()
    for step in range(1, groups):
        peer = lax.rem(q + step, groups)
        pltpu.make_async_remote_copy(
            src_ref=part_of(peer), dst_ref=levels_buf.at[peer],
            send_sem=lev_send.at[peer], recv_sem=lev_recv.at[peer],
            device_id=(peer, w), device_id_type=pl.DeviceIdType.MESH,
        ).wait_recv()

    level_count = groups * lev_rows
    coef = levels_buf[...].reshape(level_count, columns)
    modal = jnp.dot(min_ref[...], coef, preferred_element_type=jnp.float32)
    scaled = jnp.concatenate(
        [modal[:, i * pair : (i + 1) * pair] * damp for i in range(columns // pair)], axis=1
    ).astype(jnp.bfloat16)
    solved = jnp.dot(mout_ref[...], scaled, preferred_element_type=jnp.float32).astype(jnp.bfloat16)
    solved_buf[...] = solved.reshape(groups, lev_rows, columns)

    def all_copy(peer, land):
        return pltpu.make_async_remote_copy(
            src_ref=send_buf.at[peer], dst_ref=recv_buf.at[land],
            send_sem=all_send.at[peer], recv_sem=all_recv.at[land],
            device_id=coords(peer), device_id_type=pl.DeviceIdType.MESH,
        )

    lane = iota((lev_rows, pair), 1)
    empty = jnp.zeros((2 * lev_rows, pair), jnp.bfloat16)
    for turn in range(groups):
        to = lax.rem(q + 1 + turn, groups)
        outs = []
        for f in range(fields):
            blocks = []
            for s in range(part_slots):
                at = (s * fields + f) * pair
                tile = solved_buf[to, :, at : at + pair]
                none = jnp.zeros_like(tile)
                split = [jnp.where(lane < degrees, tile, none), jnp.where(lane >= degrees, tile, none)]
                split = jnp.concatenate(split, axis=0)
                blocks.append(jnp.concatenate([split if k == s else empty for k in range(part_slots)], axis=1))
            outs.append(lax.dot_general(
                legs, jnp.concatenate(blocks, axis=0), (((1,), (1,)), ((), ())),
                preferred_element_type=jnp.float32,
            ))
        for shard in range(shards):
            at = shard * halo_rows
            message = jnp.concatenate([out[at : at + halo_rows] for out in outs], axis=0)
            send_buf[shard * groups + to] = message.astype(jnp.bfloat16)

        def start(step, carry):
            all_copy(lax.rem(w + step, shards) * groups + to, me).start()
            return carry

        lax.fori_loop(0 if turn < groups - 1 else 1, shards, start, 0)
    rows = 2 * total_slots
    row = iota((rows, total_slots), 0)
    slot = part_slots * (row % everyone) + row // (2 * everyone)
    waves = jnp.sum(jnp.where(slot == iota((rows, total_slots), 1), wm, 0.0), axis=1, keepdims=True)
    parts = ((iota((rows, 1), 0) // everyone) % 2).astype(jnp.float32)
    points = table_ref.shape[1]
    table = (trig_rows_of(waves, parts, points) * scale).astype(jnp.bfloat16)
    table_ref[...] = table
    table = table.astype(jnp.float32)
    slope = pltpu.roll(table, points - 1, 1) - pltpu.roll(table, 1, 1)
    high = slope.astype(jnp.bfloat16)
    slope_ref[:rows] = high
    slope_ref[rows:] = (slope - high.astype(jnp.float32)).astype(jnp.bfloat16)
    match = iota((limit_ref.shape[0], lat_rows), 0) == iota((limit_ref.shape[0], lat_rows), 1)
    limit = jnp.sum(jnp.where(match, points_ref[...].astype(jnp.float32), 0.0), axis=1, keepdims=True)
    limit_ref[...] = jnp.broadcast_to(limit, limit_ref.shape).astype(jnp.int32)
    pairs = [(table_ref, table_hbm), (slope_ref, slope_hbm), (limit_ref, limit_hbm)]
    outputs = [pltpu.make_async_copy(a, b, out_sem.at[i]) for i, (a, b) in enumerate(pairs)]
    for copy in outputs:
        copy.start()

    mine = pltpu.make_async_copy(send_buf.at[me], recv_buf.at[me], own_sem.at[1])
    mine.start()
    mine.wait()

    def finish(step, carry):
        peer = lax.rem(me + step, everyone)
        all_copy(peer, peer).wait_recv()
        return carry

    lax.fori_loop(1, everyone, finish, 0)
    message = fields * halo_rows
    wide[...] = recv_buf[...].reshape(everyone * message, rows).astype(jnp.float32)
    lane = iota((lev_rows, rows), 1) // everyone
    count = rows // everyone
    for first in range(0, message, count):
        stack = [wide[pl.ds(first + j, everyone, stride=message), :] for j in range(count)]
        turned = jnp.concatenate(stack, axis=0).T
        for j in range(count):
            value = None
            for g in range(count):
                part = turned[g * lev_rows : (g + 1) * lev_rows]
                if g != j:
                    part = pltpu.roll(part, ((g - j) * everyone) % rows, 1)
                value = part if value is None else jnp.where(lane == g, part, value)
            f, t = divmod(first + j, halo_rows)
            bands_ref[t, f] = value.astype(jnp.bfloat16)

    def sent(step, carry):
        all_copy(lax.rem(me + step, everyone), me).wait_send()
        return carry

    lax.fori_loop(1, everyone, sent, 0)
    for step in range(1, groups):
        lev_copy(step).wait_send()
    for copy in outputs:
        copy.wait()


def section_kernel(scale, limit_ref, bands_ref, table_ref, slope_ref, out_ref, grid_buf, lon_buf, first_buf):
    halo_rows, fields, chunk, depth = bands_ref.shape
    lat_rows, width = out_ref.shape[2], out_ref.shape[3]
    inner = [halo_rows - 1] + list(range(lat_rows + 1))

    def product(a, b):
        value = jnp.dot(a, b, preferred_element_type=jnp.float32)
        return (value if scale is None else value * scale).reshape(fields, chunk, width)

    for t in range(halo_rows):
        part = bands_ref[t].reshape(fields * chunk, depth)
        grid_buf[t] = product(part, table_ref[...])
        if t in inner:
            lon_buf[t] = product(jnp.concatenate([part, part], axis=1), slope_ref[...])

    def around(ref, t, f):
        return ref[(t + 1) % halo_rows, f] - ref[(t - 1) % halo_rows, f]

    for t in inner:
        east, north = grid_buf[t, 0] * (0.5 * time_step), grid_buf[t, 1] * (0.5 * time_step)
        for f in range(fields):
            first_buf[t, f] = grid_buf[t, f] - (east * lon_buf[t, f] + north * around(grid_buf, t, f))
    column = iota((chunk, width), 1)
    for t in range(lat_rows):
        east, north = first_buf[t, 0] * (0.25 * time_step), first_buf[t, 1] * (0.25 * time_step)
        keep = column < limit_ref[t : t + 1, :1]
        for f in range(fields):
            value = first_buf[t, f]
            lon = pltpu.roll(value, width - 1, 1) - pltpu.roll(value, 1, 1)
            second = 0.5 * (grid_buf[t, f] + value) - (east * lon + north * around(first_buf, t, f))
            out_ref[f, :, t, :] = jnp.where(keep, second, 0.0)


def per_device(spectral, modes_in, modes_out, mode_depth, legendre, wave_map, row_points):
    lev_rows, slots, fields, _, degrees = spectral.shape
    groups, shards = lax.axis_size("lev"), lax.axis_size("wave")
    lat_total = legendre.shape[2]
    lat_rows = lat_total // shards
    everyone, halo_rows = groups * shards, 8
    part_slots = slots // groups
    rows = 2 * shards * slots
    fits = slots == 2 * groups and 2 * degrees == 128 and lat_rows == 4
    fits = fits and lev_rows == 32 and everyone == 32 and rows == 128
    if not fits:
        return general_path(spectral, modes_in, modes_out, mode_depth, legendre, wave_map, row_points)
    norm = 1.0 / math.sqrt(shards * slots)
    exact = math.frexp(norm)[0] == 0.5
    columns = part_slots * fields * 2 * degrees
    modes = modes_in.shape[0]
    x = spectral.reshape(lev_rows, groups * columns)
    dims = (groups, shards, slots, lev_rows, fields, degrees, lat_total, norm if exact else 1.0)
    vmem = pl.BlockSpec(memory_space=pltpu.VMEM)
    hbm = pl.BlockSpec(memory_space=pltpu.HBM)
    message = fields * halo_rows
    bf16 = jnp.bfloat16
    bands, table, slope, limit = pl.pallas_call(
        functools.partial(exchange_kernel, dims),
        out_shape=(
            jax.ShapeDtypeStruct((halo_rows, fields, lev_rows, rows), bf16),
            jax.ShapeDtypeStruct((rows, LON), bf16),
            jax.ShapeDtypeStruct((2 * rows, LON), bf16),
            jax.ShapeDtypeStruct((8, 128), jnp.int32),
        ),
        in_specs=[hbm] * 7,
        out_specs=(vmem, hbm, hbm, hbm),
        scratch_shapes=[
            pltpu.VMEM((rows, LON), bf16),
            pltpu.VMEM((2 * rows, LON), bf16),
            pltpu.VMEM((8, 128), jnp.int32),
            pltpu.VMEM((modes, modes), bf16),
            pltpu.VMEM((modes, modes), bf16),
            pltpu.VMEM((1, modes), jnp.float32),
            pltpu.VMEM((part_slots, lat_total, degrees), bf16),
            pltpu.VMEM((1, shards * slots), jnp.int32),
            pltpu.VMEM((1, lat_rows), jnp.int32),
            pltpu.VMEM((groups, lev_rows, columns), bf16),
            pltpu.VMEM((groups, lev_rows, columns), bf16),
            pltpu.VMEM((everyone, message, rows), bf16),
            pltpu.VMEM((everyone, message, rows), bf16),
            pltpu.VMEM((everyone * message, rows), jnp.float32),
            pltpu.SemaphoreType.DMA((6,)),
            pltpu.SemaphoreType.DMA((3,)),
            pltpu.SemaphoreType.DMA((2,)),
            pltpu.SemaphoreType.DMA((groups,)),
            pltpu.SemaphoreType.DMA((groups,)),
            pltpu.SemaphoreType.DMA((everyone,)),
            pltpu.SemaphoreType.DMA((everyone,)),
        ],
        compiler_params=pltpu.CompilerParams(
            collective_id=0, has_side_effects=True, vmem_limit_bytes=60 * 1024 * 1024
        ),
        name="exchange",
    )(
        x, modes_in, modes_out, mode_depth.reshape(1, -1), jnp.swapaxes(legendre, 1, 2),
        wave_map.reshape(1, -1), row_points.reshape(1, -1),
    )
    chunk = 16
    return pl.pallas_call(
        functools.partial(section_kernel, None if exact else norm),
        grid=(lev_rows // chunk,),
        out_shape=jax.ShapeDtypeStruct((fields, lev_rows, lat_rows, LON), jnp.float32),
        in_specs=[
            pl.BlockSpec((8, 128), lambda i: (0, 0)),
            pl.BlockSpec((halo_rows, fields, chunk, rows), lambda i: (0, 0, i, 0)),
            pl.BlockSpec((rows, LON), lambda i: (0, 0)),
            pl.BlockSpec((2 * rows, LON), lambda i: (0, 0)),
        ],
        out_specs=pl.BlockSpec((fields, chunk, lat_rows, LON), lambda i: (0, i, 0, 0)),
        scratch_shapes=[pltpu.VMEM((halo_rows, fields, chunk, LON), jnp.float32)] * 3,
        compiler_params=pltpu.CompilerParams(vmem_limit_bytes=60 * 1024 * 1024),
        name="sections",
    )(limit, bands, table, slope)


def solution(mesh):
    in_specs = (
        P("lev", "wave", None, None, None),
        P(),
        P(),
        P(),
        P("wave", None, None),
        P(),
        P("wave"),
    )
    out_specs = P(None, "lev", "wave", None)
    return jax.shard_map(
        per_device, mesh=mesh, in_specs=in_specs, out_specs=out_specs, check_vma=False
    )
```

```python
import functools
import math

import jax
import jax.numpy as jnp
from jax import lax
from jax.experimental import pallas as pl
from jax.experimental.pallas import tpu as pltpu
from jax.sharding import PartitionSpec as P

LON = 1280


time_step = 0.8


def with_halo(value, sides, width):
    for axis, dim in sides:
        size, length = (lax.axis_size(axis), value.shape[dim])
        up = [(i, (i + 1) % size) for i in range(size - 1)]
        down = [(j, i) for i, j in up]
        last = lax.slice_in_dim(value, length - width, length, axis=dim)
        leading = lax.slice_in_dim(value, 0, width, axis=dim)
        before = lax.ppermute(last, axis, up)
        after = lax.ppermute(leading, axis, down)
        value = jnp.concatenate([before, value, after], axis=dim)
    return value


def damping(mode_depth, degree_of, degree_total):
    ratio = degree_of * (degree_of + 1.0) / float(degree_total * degree_total)
    return 1.0 / (1.0 + mode_depth[:, None] * ratio[None, :])


def trig_table(wave_map, lon_count):
    column = jnp.arange(lon_count, dtype=jnp.int32)
    product = wave_map[:, None] * column[None, :] % lon_count
    angles = product.astype(jnp.float32) * (2.0 * math.pi / lon_count)
    return jnp.stack([jnp.cos(angles), -jnp.sin(angles)], axis=1).astype(jnp.bfloat16)


def tendency(fields_ext):
    center = fields_ext[..., 1:-1, :]
    ahead_lon = jnp.roll(center, -1, axis=-1)
    behind_lon = jnp.roll(center, 1, axis=-1)
    ahead_lat = fields_ext[..., 2:, :]
    behind_lat = fields_ext[..., :-2, :]
    return center[0] * (ahead_lon - behind_lon) * 0.5 + center[1] * (ahead_lat - behind_lat) * 0.5


def legendre_rows(solved, legendre):
    band_rows = jnp.einsum(
        "lsfcn,snt->tlsfc", solved, legendre, preferred_element_type=jnp.float32
    ).astype(jnp.bfloat16)
    return band_rows.reshape(band_rows.shape[0], -1)


def general_path(spectral, modes_in, modes_out, mode_depth, legendre, wave_map, row_points):
    lev_rows = spectral.shape[0]
    wave_slots = spectral.shape[1]
    field_count = spectral.shape[2]
    degree_count = spectral.shape[4]
    shard_count = lax.axis_size("wave")
    first_slot = lax.axis_index("wave") * wave_slots
    local_waves = lax.dynamic_slice_in_dim(wave_map, first_slot, wave_slots)
    degrees = jnp.arange(degree_count, dtype=jnp.int32)
    keep_mask = degrees[None, :] >= local_waves[:, None]
    masked = jnp.where(keep_mask[None, :, None, None, :], spectral, jnp.zeros_like(spectral))
    flattened = masked.reshape(lev_rows, -1)
    trig_rows = trig_table(wave_map, LON).reshape(shard_count, wave_slots, 2, LON)
    norm_factor = 1.0 / math.sqrt(wave_map.shape[0])
    modal_part = jnp.dot(
        modes_in,
        lax.all_gather(flattened, "lev", axis=0, tiled=True),
        preferred_element_type=jnp.float32,
    )
    degree_of = (jnp.arange(flattened.shape[1], dtype=jnp.int32) % degree_count).astype(jnp.float32)
    scaled = (modal_part * damping(mode_depth, degree_of, degree_count)).astype(jnp.bfloat16)
    own_rows = lax.dynamic_slice_in_dim(modes_out, lax.axis_index("lev") * lev_rows, lev_rows, 0)
    solved = jnp.dot(own_rows, scaled, preferred_element_type=jnp.float32).astype(jnp.bfloat16)
    band_rows = legendre_rows(solved.reshape(spectral.shape), legendre)
    regrouped = lax.all_to_all(band_rows, "wave", split_axis=0, concat_axis=1, tiled=True)
    lat_rows = regrouped.shape[0]
    split_bands = regrouped.reshape(lat_rows, shard_count, lev_rows, wave_slots, field_count, 2)
    grid_field = (
        jnp.einsum("twlsfc,wscx->fltx", split_bands, trig_rows, preferred_element_type=jnp.float32)
        * norm_factor
    )
    wide_rows = with_halo(grid_field, (("wave", 2),), 2)
    section_wide = wide_rows[:, :, 1:-1, :] - time_step * tendency(wide_rows)
    second = 0.5 * (grid_field + section_wide[:, :, 1:-1, :] - time_step * tendency(section_wide))
    points = jnp.arange(LON, dtype=jnp.int32)[None, :] < row_points[:, None]
    return jnp.where(points[None, None, :, :], second, jnp.zeros_like(second))


def iota(shape, dim):
    return lax.broadcasted_iota(jnp.int32, shape, dim)


def trig_rows_of(waves, parts, points):
    rows = waves.shape[0]
    column = iota((rows, points), 1).astype(jnp.float32)
    product = waves * column + parts * (points / 4)
    turns = product * (1.0 / points)
    left = product - jnp.floor(turns) * points
    folded = 0.25 - jnp.abs(left * (1.0 / points) - 0.5)
    angle = folded * (2.0 * math.pi)
    square = angle * angle
    total = jnp.full_like(angle, -1.0 / math.factorial(11))
    for order in (9, 7, 5, 3, 1):
        sign = 1.0 if order % 4 == 1 else -1.0
        total = total * square + sign / math.factorial(order)
    return -(total * angle)


def exchange_kernel(
    dims, x_ref, min_hbm, mout_hbm, depth_hbm, leg_hbm, wm_hbm, points_hbm,
    bands_ref, table_hbm, slope_hbm, limit_hbm,
    table_ref, slope_ref, limit_ref, min_ref, mout_ref, depth_ref, leg_ref, wm_ref, points_ref,
    levels_buf, solved_buf, send_buf, recv_buf, wide,
    in_sem, out_sem, own_sem, lev_send, lev_recv, all_send, all_recv,
):
    groups, shards, slots, lev_rows, fields, degrees, lat_total, scale = dims
    halo_rows = 8
    lat_rows = lat_total // shards
    part_slots = slots // groups
    everyone = groups * shards
    q = lax.axis_index("lev")
    w = lax.axis_index("wave")
    me = w * groups + q

    def coords(place):
        return (lax.rem(place, groups), lax.div(place, groups))

    barrier = pltpu.get_barrier_semaphore()

    def greet(step, carry):
        place = lax.rem(me + step, everyone)
        pl.semaphore_signal(barrier, inc=1, device_id=coords(place), device_id_type=pl.DeviceIdType.MESH)
        return carry

    lax.fori_loop(1, everyone, greet, 0)

    pairs = [
        (wm_hbm, wm_ref), (leg_hbm.at[pl.ds(q * part_slots, part_slots)], leg_ref),
        (depth_hbm, depth_ref), (points_hbm, points_ref), (min_hbm, min_ref), (mout_hbm, mout_ref),
    ]
    inputs = [pltpu.make_async_copy(a, b, in_sem.at[i]) for i, (a, b) in enumerate(pairs)]
    for copy in inputs:
        copy.start()
    columns = levels_buf.shape[2]

    def part_of(peer):
        return x_ref.at[:, pl.ds(pl.multiple_of(peer * columns, 128), columns)]

    own = pltpu.make_async_copy(part_of(q), levels_buf.at[q], own_sem.at[0])
    own.start()

    for copy in inputs:
        copy.wait()

    total_slots = shards * slots
    wm = wm_ref[...].astype(jnp.float32)
    pair = 2 * degrees
    halo_total = shards * halo_rows
    row = iota((halo_total, lat_total), 0)
    inner = row % halo_rows
    lat = (row // halo_rows) * lat_rows + jnp.where(inner < halo_rows - 2, inner, inner - halo_rows)
    pick = (lat == iota((halo_total, lat_total), 1)).astype(jnp.float32).astype(jnp.bfloat16)
    double = (iota((degrees, pair), 0) == iota((degrees, pair), 1) % degrees)
    double = double.astype(jnp.float32).astype(jnp.bfloat16)
    degree = (iota((halo_total, pair), 1) % degrees).astype(jnp.float32)
    legs = []
    for s in range(part_slots):
        leg = jnp.dot(leg_ref[s], double, preferred_element_type=jnp.float32)
        leg = jnp.dot(pick, leg.astype(jnp.bfloat16), preferred_element_type=jnp.float32)
        place = w * slots + q * part_slots + s
        chosen = iota((1, total_slots), 1) == place
        wave = jnp.sum(jnp.where(chosen, wm, 0.0), axis=1, keepdims=True)
        legs.append(jnp.where(degree >= wave, leg, 0.0).astype(jnp.bfloat16))
    legs = jnp.concatenate(legs, axis=1)
    modes = min_ref.shape[0]
    eye = iota((modes, modes), 0) == iota((modes, modes), 1)
    depth = jnp.sum(jnp.where(eye, depth_ref[...], 0.0), axis=1, keepdims=True)
    degree_row = (iota((modes, pair), 1) % degrees).astype(jnp.float32)
    ratio = degree_row * (degree_row + 1.0) / float(degrees * degrees)
    damp = 1.0 / (1.0 + depth * ratio)

    pl.semaphore_wait(barrier, everyone - 1)

    def lev_copy(step):
        peer = lax.rem(q + step, groups)
        return pltpu.make_async_remote_copy(
            src_ref=part_of(peer), dst_ref=levels_buf.at[q],
            send_sem=lev_send.at[peer], recv_sem=lev_recv.at[q],
            device_id=(peer, w), device_id_type=pl.DeviceIdType.MESH,
        )

    for step in range(1, groups):
        lev_copy(step).start()
    own.wait()
    for step in range(1, groups):
        peer = lax.rem(q + step, groups)
        pltpu.make_async_remote_copy(
            src_ref=part_of(peer), dst_ref=levels_buf.at[peer],
            send_sem=lev_send.at[peer], recv_sem=lev_recv.at[peer],
            device_id=(peer, w), device_id_type=pl.DeviceIdType.MESH,
        ).wait_recv()

    level_count = groups * lev_rows
    coef = levels_buf[...].reshape(level_count, columns)
    modal = jnp.dot(min_ref[...], coef, preferred_element_type=jnp.float32)
    scaled = jnp.concatenate(
        [modal[:, i * pair : (i + 1) * pair] * damp for i in range(columns // pair)], axis=1
    ).astype(jnp.bfloat16)
    solved = jnp.dot(mout_ref[...], scaled, preferred_element_type=jnp.float32).astype(jnp.bfloat16)
    solved_buf[...] = solved.reshape(groups, lev_rows, columns)

    def all_copy(peer, land):
        return pltpu.make_async_remote_copy(
            src_ref=send_buf.at[peer], dst_ref=recv_buf.at[land],
            send_sem=all_send.at[peer], recv_sem=all_recv.at[land],
            device_id=coords(peer), device_id_type=pl.DeviceIdType.MESH,
        )

    lane = iota((lev_rows, pair), 1)
    empty = jnp.zeros((2 * lev_rows, pair), jnp.bfloat16)
    for turn in range(groups):
        to = lax.rem(q + 1 + turn, groups)
        outs = []
        for f in range(fields):
            blocks = []
            for s in range(part_slots):
                at = (s * fields + f) * pair
                tile = solved_buf[to, :, at : at + pair]
                none = jnp.zeros_like(tile)
                split = [jnp.where(lane < degrees, tile, none), jnp.where(lane >= degrees, tile, none)]
                split = jnp.concatenate(split, axis=0)
                blocks.append(jnp.concatenate([split if k == s else empty for k in range(part_slots)], axis=1))
            outs.append(lax.dot_general(
                legs, jnp.concatenate(blocks, axis=0), (((1,), (1,)), ((), ())),
                preferred_element_type=jnp.float32,
            ))
        for shard in range(shards):
            at = shard * halo_rows
            message = jnp.concatenate([out[at : at + halo_rows] for out in outs], axis=0)
            send_buf[shard * groups + to] = message.astype(jnp.bfloat16)

        def start(step, carry):
            all_copy(lax.rem(w + step, shards) * groups + to, me).start()
            return carry

        lax.fori_loop(0 if turn < groups - 1 else 1, shards, start, 0)
    rows = 2 * total_slots
    row = iota((rows, total_slots), 0)
    slot = part_slots * (row % everyone) + row // (2 * everyone)
    waves = jnp.sum(jnp.where(slot == iota((rows, total_slots), 1), wm, 0.0), axis=1, keepdims=True)
    parts = ((iota((rows, 1), 0) // everyone) % 2).astype(jnp.float32)
    points = table_ref.shape[1]
    table = (trig_rows_of(waves, parts, points) * scale).astype(jnp.bfloat16)
    table_ref[...] = table
    table = table.astype(jnp.float32)
    slope = pltpu.roll(table, points - 1, 1) - pltpu.roll(table, 1, 1)
    high = slope.astype(jnp.bfloat16)
    slope_ref[:rows] = high
    slope_ref[rows:] = (slope - high.astype(jnp.float32)).astype(jnp.bfloat16)
    match = iota((limit_ref.shape[0], lat_rows), 0) == iota((limit_ref.shape[0], lat_rows), 1)
    limit = jnp.sum(jnp.where(match, points_ref[...].astype(jnp.float32), 0.0), axis=1, keepdims=True)
    limit_ref[...] = jnp.broadcast_to(limit, limit_ref.shape).astype(jnp.int32)
    pairs = [(table_ref, table_hbm), (slope_ref, slope_hbm), (limit_ref, limit_hbm)]
    outputs = [pltpu.make_async_copy(a, b, out_sem.at[i]) for i, (a, b) in enumerate(pairs)]
    for copy in outputs:
        copy.start()

    mine = pltpu.make_async_copy(send_buf.at[me], recv_buf.at[me], own_sem.at[1])
    mine.start()
    mine.wait()

    def finish(step, carry):
        peer = lax.rem(me + step, everyone)
        all_copy(peer, peer).wait_recv()
        return carry

    lax.fori_loop(1, everyone, finish, 0)
    message = fields * halo_rows
    wide[...] = recv_buf[...].reshape(everyone * message, rows).astype(jnp.float32)
    lane = iota((lev_rows, rows), 1) // everyone
    count = rows // everyone
    for first in range(0, message, count):
        stack = [wide[pl.ds(first + j, everyone, stride=message), :] for j in range(count)]
        turned = jnp.concatenate(stack, axis=0).T
        for j in range(count):
            value = None
            for g in range(count):
                part = turned[g * lev_rows : (g + 1) * lev_rows]
                if g != j:
                    part = pltpu.roll(part, ((g - j) * everyone) % rows, 1)
                value = part if value is None else jnp.where(lane == g, part, value)
            f, t = divmod(first + j, halo_rows)
            bands_ref[t, f] = value.astype(jnp.bfloat16)

    def sent(step, carry):
        all_copy(lax.rem(me + step, everyone), me).wait_send()
        return carry

    lax.fori_loop(1, everyone, sent, 0)
    for step in range(1, groups):
        lev_copy(step).wait_send()
    for copy in outputs:
        copy.wait()


def section_kernel(scale, limit_ref, bands_ref, table_ref, slope_ref, out_ref, grid_buf, lon_buf, first_buf):
    halo_rows, fields, chunk, depth = bands_ref.shape
    lat_rows, width = out_ref.shape[2], out_ref.shape[3]
    inner = [halo_rows - 1] + list(range(lat_rows + 1))

    def product(a, b):
        value = jnp.dot(a, b, preferred_element_type=jnp.float32)
        return (value if scale is None else value * scale).reshape(grid_buf.shape)

    part = bands_ref[...].reshape(halo_rows * fields * chunk, depth)
    grid_buf[...] = product(part, table_ref[...])
    lon_buf[...] = product(jnp.concatenate([part, part], axis=1), slope_ref[...])

    def around(ref, t, f):
        return ref[(t + 1) % halo_rows, f] - ref[(t - 1) % halo_rows, f]

    for t in inner:
        east, north = grid_buf[t, 0] * (0.5 * time_step), grid_buf[t, 1] * (0.5 * time_step)
        for f in range(fields):
            first_buf[t, f] = grid_buf[t, f] - (east * lon_buf[t, f] + north * around(grid_buf, t, f))
    column = iota((chunk, width), 1)
    for t in range(lat_rows):
        east, north = first_buf[t, 0] * (0.25 * time_step), first_buf[t, 1] * (0.25 * time_step)
        keep = column < limit_ref[t : t + 1, :1]
        for f in range(fields):
            value = first_buf[t, f]
            lon = pltpu.roll(value, width - 1, 1) - pltpu.roll(value, 1, 1)
            second = 0.5 * (grid_buf[t, f] + value) - (east * lon + north * around(first_buf, t, f))
            out_ref[f, :, t, :] = jnp.where(keep, second, 0.0)


def per_device(spectral, modes_in, modes_out, mode_depth, legendre, wave_map, row_points):
    lev_rows, slots, fields, _, degrees = spectral.shape
    groups, shards = lax.axis_size("lev"), lax.axis_size("wave")
    lat_total = legendre.shape[2]
    lat_rows = lat_total // shards
    everyone, halo_rows = groups * shards, 8
    part_slots = slots // groups
    rows = 2 * shards * slots
    fits = slots == 2 * groups and 2 * degrees == 128 and lat_rows == 4
    fits = fits and lev_rows == 32 and everyone == 32 and rows == 128
    if not fits:
        return general_path(spectral, modes_in, modes_out, mode_depth, legendre, wave_map, row_points)
    norm = 1.0 / math.sqrt(shards * slots)
    exact = math.frexp(norm)[0] == 0.5
    columns = part_slots * fields * 2 * degrees
    modes = modes_in.shape[0]
    x = spectral.reshape(lev_rows, groups * columns)
    dims = (groups, shards, slots, lev_rows, fields, degrees, lat_total, norm if exact else 1.0)
    vmem = pl.BlockSpec(memory_space=pltpu.VMEM)
    hbm = pl.BlockSpec(memory_space=pltpu.HBM)
    message = fields * halo_rows
    bf16 = jnp.bfloat16
    bands, table, slope, limit = pl.pallas_call(
        functools.partial(exchange_kernel, dims),
        out_shape=(
            jax.ShapeDtypeStruct((halo_rows, fields, lev_rows, rows), bf16),
            jax.ShapeDtypeStruct((rows, LON), bf16),
            jax.ShapeDtypeStruct((2 * rows, LON), bf16),
            jax.ShapeDtypeStruct((8, 128), jnp.int32),
        ),
        in_specs=[hbm] * 7,
        out_specs=(vmem, hbm, hbm, hbm),
        scratch_shapes=[
            pltpu.VMEM((rows, LON), bf16),
            pltpu.VMEM((2 * rows, LON), bf16),
            pltpu.VMEM((8, 128), jnp.int32),
            pltpu.VMEM((modes, modes), bf16),
            pltpu.VMEM((modes, modes), bf16),
            pltpu.VMEM((1, modes), jnp.float32),
            pltpu.VMEM((part_slots, lat_total, degrees), bf16),
            pltpu.VMEM((1, shards * slots), jnp.int32),
            pltpu.VMEM((1, lat_rows), jnp.int32),
            pltpu.VMEM((groups, lev_rows, columns), bf16),
            pltpu.VMEM((groups, lev_rows, columns), bf16),
            pltpu.VMEM((everyone, message, rows), bf16),
            pltpu.VMEM((everyone, message, rows), bf16),
            pltpu.VMEM((everyone * message, rows), jnp.float32),
            pltpu.SemaphoreType.DMA((6,)),
            pltpu.SemaphoreType.DMA((3,)),
            pltpu.SemaphoreType.DMA((2,)),
            pltpu.SemaphoreType.DMA((groups,)),
            pltpu.SemaphoreType.DMA((groups,)),
            pltpu.SemaphoreType.DMA((everyone,)),
            pltpu.SemaphoreType.DMA((everyone,)),
        ],
        compiler_params=pltpu.CompilerParams(
            collective_id=0, has_side_effects=True, vmem_limit_bytes=60 * 1024 * 1024
        ),
        name="exchange",
    )(
        x, modes_in, modes_out, mode_depth.reshape(1, -1), jnp.swapaxes(legendre, 1, 2),
        wave_map.reshape(1, -1), row_points.reshape(1, -1),
    )
    chunk = 16
    return pl.pallas_call(
        functools.partial(section_kernel, None if exact else norm),
        grid=(lev_rows // chunk,),
        out_shape=jax.ShapeDtypeStruct((fields, lev_rows, lat_rows, LON), jnp.float32),
        in_specs=[
            pl.BlockSpec((8, 128), lambda i: (0, 0)),
            pl.BlockSpec((halo_rows, fields, chunk, rows), lambda i: (0, 0, i, 0)),
            pl.BlockSpec((rows, LON), lambda i: (0, 0)),
            pl.BlockSpec((2 * rows, LON), lambda i: (0, 0)),
        ],
        out_specs=pl.BlockSpec((fields, chunk, lat_rows, LON), lambda i: (0, i, 0, 0)),
        scratch_shapes=[pltpu.VMEM((halo_rows, fields, chunk, LON), jnp.float32)] * 3,
        compiler_params=pltpu.CompilerParams(vmem_limit_bytes=60 * 1024 * 1024),
        name="sections",
    )(limit, bands, table, slope)


def solution(mesh):
    in_specs = (
        P("lev", "wave", None, None, None),
        P(),
        P(),
        P(),
        P("wave", None, None),
        P(),
        P("wave"),
    )
    out_specs = P(None, "lev", "wave", None)
    return jax.shard_map(
        per_device, mesh=mesh, in_specs=in_specs, out_specs=out_specs, check_vma=False
    )
```

```python
import functools
import math

import jax
import jax.numpy as jnp
from jax import lax
from jax.experimental import pallas as pl
from jax.experimental.pallas import tpu as pltpu
from jax.sharding import PartitionSpec as P

LON = 1280


time_step = 0.8


def with_halo(value, sides, width):
    for axis, dim in sides:
        size, length = (lax.axis_size(axis), value.shape[dim])
        up = [(i, (i + 1) % size) for i in range(size - 1)]
        down = [(j, i) for i, j in up]
        last = lax.slice_in_dim(value, length - width, length, axis=dim)
        leading = lax.slice_in_dim(value, 0, width, axis=dim)
        before = lax.ppermute(last, axis, up)
        after = lax.ppermute(leading, axis, down)
        value = jnp.concatenate([before, value, after], axis=dim)
    return value


def damping(mode_depth, degree_of, degree_total):
    ratio = degree_of * (degree_of + 1.0) / float(degree_total * degree_total)
    return 1.0 / (1.0 + mode_depth[:, None] * ratio[None, :])


def trig_table(wave_map, lon_count):
    column = jnp.arange(lon_count, dtype=jnp.int32)
    product = wave_map[:, None] * column[None, :] % lon_count
    angles = product.astype(jnp.float32) * (2.0 * math.pi / lon_count)
    return jnp.stack([jnp.cos(angles), -jnp.sin(angles)], axis=1).astype(jnp.bfloat16)


def tendency(fields_ext):
    center = fields_ext[..., 1:-1, :]
    ahead_lon = jnp.roll(center, -1, axis=-1)
    behind_lon = jnp.roll(center, 1, axis=-1)
    ahead_lat = fields_ext[..., 2:, :]
    behind_lat = fields_ext[..., :-2, :]
    return center[0] * (ahead_lon - behind_lon) * 0.5 + center[1] * (ahead_lat - behind_lat) * 0.5


def legendre_rows(solved, legendre):
    band_rows = jnp.einsum(
        "lsfcn,snt->tlsfc", solved, legendre, preferred_element_type=jnp.float32
    ).astype(jnp.bfloat16)
    return band_rows.reshape(band_rows.shape[0], -1)


def general_path(spectral, modes_in, modes_out, mode_depth, legendre, wave_map, row_points):
    lev_rows = spectral.shape[0]
    wave_slots = spectral.shape[1]
    field_count = spectral.shape[2]
    degree_count = spectral.shape[4]
    shard_count = lax.axis_size("wave")
    first_slot = lax.axis_index("wave") * wave_slots
    local_waves = lax.dynamic_slice_in_dim(wave_map, first_slot, wave_slots)
    degrees = jnp.arange(degree_count, dtype=jnp.int32)
    keep_mask = degrees[None, :] >= local_waves[:, None]
    masked = jnp.where(keep_mask[None, :, None, None, :], spectral, jnp.zeros_like(spectral))
    flattened = masked.reshape(lev_rows, -1)
    trig_rows = trig_table(wave_map, LON).reshape(shard_count, wave_slots, 2, LON)
    norm_factor = 1.0 / math.sqrt(wave_map.shape[0])
    modal_part = jnp.dot(
        modes_in,
        lax.all_gather(flattened, "lev", axis=0, tiled=True),
        preferred_element_type=jnp.float32,
    )
    degree_of = (jnp.arange(flattened.shape[1], dtype=jnp.int32) % degree_count).astype(jnp.float32)
    scaled = (modal_part * damping(mode_depth, degree_of, degree_count)).astype(jnp.bfloat16)
    own_rows = lax.dynamic_slice_in_dim(modes_out, lax.axis_index("lev") * lev_rows, lev_rows, 0)
    solved = jnp.dot(own_rows, scaled, preferred_element_type=jnp.float32).astype(jnp.bfloat16)
    band_rows = legendre_rows(solved.reshape(spectral.shape), legendre)
    regrouped = lax.all_to_all(band_rows, "wave", split_axis=0, concat_axis=1, tiled=True)
    lat_rows = regrouped.shape[0]
    split_bands = regrouped.reshape(lat_rows, shard_count, lev_rows, wave_slots, field_count, 2)
    grid_field = (
        jnp.einsum("twlsfc,wscx->fltx", split_bands, trig_rows, preferred_element_type=jnp.float32)
        * norm_factor
    )
    wide_rows = with_halo(grid_field, (("wave", 2),), 2)
    section_wide = wide_rows[:, :, 1:-1, :] - time_step * tendency(wide_rows)
    second = 0.5 * (grid_field + section_wide[:, :, 1:-1, :] - time_step * tendency(section_wide))
    points = jnp.arange(LON, dtype=jnp.int32)[None, :] < row_points[:, None]
    return jnp.where(points[None, None, :, :], second, jnp.zeros_like(second))


def iota(shape, dim):
    return lax.broadcasted_iota(jnp.int32, shape, dim)


def trig_rows_of(waves, parts, points):
    rows = waves.shape[0]
    column = iota((rows, points), 1).astype(jnp.float32)
    product = waves * column + parts * (points / 4)
    turns = product * (1.0 / points)
    left = product - jnp.floor(turns) * points
    folded = 0.25 - jnp.abs(left * (1.0 / points) - 0.5)
    angle = folded * (2.0 * math.pi)
    square = angle * angle
    total = jnp.full_like(angle, -1.0 / math.factorial(11))
    for order in (9, 7, 5, 3, 1):
        sign = 1.0 if order % 4 == 1 else -1.0
        total = total * square + sign / math.factorial(order)
    return -(total * angle)


def exchange_kernel(
    dims, x_ref, min_hbm, mout_hbm, depth_hbm, leg_hbm, wm_hbm, points_hbm,
    bands_ref, table_hbm, slope_hbm, limit_hbm,
    table_ref, slope_ref, limit_ref, min_ref, mout_ref, depth_ref, leg_ref, wm_ref, points_ref,
    levels_buf, solved_buf, send_buf, recv_buf, wide,
    in_sem, out_sem, own_sem, lev_send, lev_recv, all_send, all_recv,
):
    groups, shards, slots, lev_rows, fields, degrees, lat_total, scale = dims
    halo_rows = 8
    lat_rows = lat_total // shards
    part_slots = slots // groups
    everyone = groups * shards
    q = lax.axis_index("lev")
    w = lax.axis_index("wave")
    me = w * groups + q

    def coords(place):
        return (lax.rem(place, groups), lax.div(place, groups))

    barrier = pltpu.get_barrier_semaphore()

    def greet(step, carry):
        place = lax.rem(me + step, everyone)
        pl.semaphore_signal(barrier, inc=1, device_id=coords(place), device_id_type=pl.DeviceIdType.MESH)
        return carry

    lax.fori_loop(1, everyone, greet, 0)

    pairs = [
        (wm_hbm, wm_ref), (leg_hbm.at[pl.ds(q * part_slots, part_slots)], leg_ref),
        (depth_hbm, depth_ref), (points_hbm, points_ref), (min_hbm, min_ref), (mout_hbm, mout_ref),
    ]
    inputs = [pltpu.make_async_copy(a, b, in_sem.at[i]) for i, (a, b) in enumerate(pairs)]
    for copy in inputs:
        copy.start()
    columns = levels_buf.shape[2]

    def part_of(peer):
        return x_ref.at[:, pl.ds(pl.multiple_of(peer * columns, 128), columns)]

    own = pltpu.make_async_copy(part_of(q), levels_buf.at[q], own_sem.at[0])
    own.start()

    for copy in inputs:
        copy.wait()

    total_slots = shards * slots
    wm = wm_ref[...].astype(jnp.float32)
    pair = 2 * degrees
    halo_total = shards * halo_rows
    row = iota((halo_total, lat_total), 0)
    inner = row % halo_rows
    lat = (row // halo_rows) * lat_rows + jnp.where(inner < halo_rows - 2, inner, inner - halo_rows)
    pick = (lat == iota((halo_total, lat_total), 1)).astype(jnp.float32).astype(jnp.bfloat16)
    double = (iota((degrees, pair), 0) == iota((degrees, pair), 1) % degrees)
    double = double.astype(jnp.float32).astype(jnp.bfloat16)
    degree = (iota((halo_total, pair), 1) % degrees).astype(jnp.float32)
    legs = []
    for s in range(part_slots):
        leg = jnp.dot(leg_ref[s], double, preferred_element_type=jnp.float32)
        leg = jnp.dot(pick, leg.astype(jnp.bfloat16), preferred_element_type=jnp.float32)
        place = w * slots + q * part_slots + s
        chosen = iota((1, total_slots), 1) == place
        wave = jnp.sum(jnp.where(chosen, wm, 0.0), axis=1, keepdims=True)
        legs.append(jnp.where(degree >= wave, leg, 0.0).astype(jnp.bfloat16))
    legs = jnp.concatenate(legs, axis=1)
    modes = min_ref.shape[0]
    eye = iota((modes, modes), 0) == iota((modes, modes), 1)
    depth = jnp.sum(jnp.where(eye, depth_ref[...], 0.0), axis=1, keepdims=True)
    degree_row = (iota((modes, pair), 1) % degrees).astype(jnp.float32)
    ratio = degree_row * (degree_row + 1.0) / float(degrees * degrees)
    damp = 1.0 / (1.0 + depth * ratio)

    pl.semaphore_wait(barrier, everyone - 1)

    def lev_copy(step):
        peer = lax.rem(q + step, groups)
        return pltpu.make_async_remote_copy(
            src_ref=part_of(peer), dst_ref=levels_buf.at[q],
            send_sem=lev_send.at[peer], recv_sem=lev_recv.at[q],
            device_id=(peer, w), device_id_type=pl.DeviceIdType.MESH,
        )

    for step in range(1, groups):
        lev_copy(step).start()
    own.wait()
    for step in range(1, groups):
        peer = lax.rem(q + step, groups)
        pltpu.make_async_remote_copy(
            src_ref=part_of(peer), dst_ref=levels_buf.at[peer],
            send_sem=lev_send.at[peer], recv_sem=lev_recv.at[peer],
            device_id=(peer, w), device_id_type=pl.DeviceIdType.MESH,
        ).wait_recv()

    level_count = groups * lev_rows
    coef = levels_buf[...].reshape(level_count, columns)
    modal = jnp.dot(min_ref[...], coef, preferred_element_type=jnp.float32)
    scaled = jnp.concatenate(
        [modal[:, i * pair : (i + 1) * pair] * damp for i in range(columns // pair)], axis=1
    ).astype(jnp.bfloat16)
    solved = jnp.dot(mout_ref[...], scaled, preferred_element_type=jnp.float32).astype(jnp.bfloat16)
    solved_buf[...] = solved.reshape(groups, lev_rows, columns)

    def all_copy(peer, land):
        return pltpu.make_async_remote_copy(
            src_ref=send_buf.at[peer], dst_ref=recv_buf.at[land],
            send_sem=all_send.at[peer], recv_sem=all_recv.at[land],
            device_id=coords(peer), device_id_type=pl.DeviceIdType.MESH,
        )

    lane = iota((lev_rows, pair), 1)
    empty = jnp.zeros((2 * lev_rows, pair), jnp.bfloat16)
    for turn in range(groups):
        to = lax.rem(q + 1 + turn, groups)
        outs = []
        for f in range(fields):
            blocks = []
            for s in range(part_slots):
                at = (s * fields + f) * pair
                tile = solved_buf[to, :, at : at + pair]
                none = jnp.zeros_like(tile)
                split = [jnp.where(lane < degrees, tile, none), jnp.where(lane >= degrees, tile, none)]
                split = jnp.concatenate(split, axis=0)
                blocks.append(jnp.concatenate([split if k == s else empty for k in range(part_slots)], axis=1))
            outs.append(lax.dot_general(
                legs, jnp.concatenate(blocks, axis=0), (((1,), (1,)), ((), ())),
                preferred_element_type=jnp.float32,
            ))
        for shard in range(shards):
            at = shard * halo_rows
            message = jnp.concatenate([out[at : at + halo_rows] for out in outs], axis=0)
            send_buf[shard * groups + to] = message.astype(jnp.bfloat16)

        def start(step, carry):
            all_copy(lax.rem(w + step, shards) * groups + to, me).start()
            return carry

        lax.fori_loop(0 if turn < groups - 1 else 1, shards, start, 0)
    rows = 2 * total_slots
    row = iota((rows, total_slots), 0)
    slot = part_slots * (row % everyone) + row // (2 * everyone)
    waves = jnp.sum(jnp.where(slot == iota((rows, total_slots), 1), wm, 0.0), axis=1, keepdims=True)
    parts = ((iota((rows, 1), 0) // everyone) % 2).astype(jnp.float32)
    points = table_ref.shape[1]
    table = (trig_rows_of(waves, parts, points) * scale).astype(jnp.bfloat16)
    table_ref[...] = table
    table = table.astype(jnp.float32)
    slope = pltpu.roll(table, points - 1, 1) - pltpu.roll(table, 1, 1)
    high = slope.astype(jnp.bfloat16)
    slope_ref[:rows] = high
    slope_ref[rows:] = (slope - high.astype(jnp.float32)).astype(jnp.bfloat16)
    match = iota((limit_ref.shape[0], lat_rows), 0) == iota((limit_ref.shape[0], lat_rows), 1)
    limit = jnp.sum(jnp.where(match, points_ref[...].astype(jnp.float32), 0.0), axis=1, keepdims=True)
    limit_ref[...] = jnp.broadcast_to(limit, limit_ref.shape).astype(jnp.int32)
    pairs = [(table_ref, table_hbm), (slope_ref, slope_hbm), (limit_ref, limit_hbm)]
    outputs = [pltpu.make_async_copy(a, b, out_sem.at[i]) for i, (a, b) in enumerate(pairs)]
    for copy in outputs:
        copy.start()

    mine = pltpu.make_async_copy(send_buf.at[me], recv_buf.at[me], own_sem.at[1])
    mine.start()
    mine.wait()

    def finish(step, carry):
        peer = lax.rem(me + step, everyone)
        all_copy(peer, peer).wait_recv()
        return carry

    lax.fori_loop(1, everyone, finish, 0)
    message = fields * halo_rows
    wide[...] = recv_buf[...].reshape(everyone * message, rows).astype(jnp.float32)
    lane = iota((lev_rows, rows), 1) // everyone
    count = rows // everyone
    for first in range(0, message, count):
        stack = [wide[pl.ds(first + j, everyone, stride=message), :] for j in range(count)]
        turned = jnp.concatenate(stack, axis=0).T
        for j in range(count):
            value = None
            for g in range(count):
                part = turned[g * lev_rows : (g + 1) * lev_rows]
                if g != j:
                    part = pltpu.roll(part, ((g - j) * everyone) % rows, 1)
                value = part if value is None else jnp.where(lane == g, part, value)
            f, t = divmod(first + j, halo_rows)
            bands_ref[t, f] = value.astype(jnp.bfloat16)

    def sent(step, carry):
        all_copy(lax.rem(me + step, everyone), me).wait_send()
        return carry

    lax.fori_loop(1, everyone, sent, 0)
    for step in range(1, groups):
        lev_copy(step).wait_send()
    for copy in outputs:
        copy.wait()


def section_kernel(scale, limit_ref, bands_ref, table_ref, slope_ref, out_ref, grid_buf, lon_buf, first_buf):
    halo_rows, fields, chunk, depth = bands_ref.shape
    lat_rows, width = out_ref.shape[2], out_ref.shape[3]
    inner = [halo_rows - 1] + list(range(lat_rows + 1))

    def product(a, b):
        value = jnp.dot(a, b, preferred_element_type=jnp.float32)
        return (value if scale is None else value * scale).reshape(grid_buf.shape)

    part = bands_ref[...].reshape(halo_rows * fields * chunk, depth)
    grid_buf[...] = product(part, table_ref[...])
    lon_buf[...] = product(jnp.concatenate([part, part], axis=1), slope_ref[...])

    def around(ref, t, f):
        return ref[(t + 1) % halo_rows, f] - ref[(t - 1) % halo_rows, f]

    for t in inner:
        east, north = grid_buf[t, 0] * (0.5 * time_step), grid_buf[t, 1] * (0.5 * time_step)
        for f in range(fields):
            first_buf[t, f] = grid_buf[t, f] - (east * lon_buf[t, f] + north * around(grid_buf, t, f))
    column = iota((chunk, width), 1)
    for t in range(lat_rows):
        east, north = first_buf[t, 0] * (0.25 * time_step), first_buf[t, 1] * (0.25 * time_step)
        keep = column < limit_ref[t : t + 1, :1]
        for f in range(fields):
            value = first_buf[t, f]
            lon = pltpu.roll(value, width - 1, 1) - pltpu.roll(value, 1, 1)
            second = 0.5 * (grid_buf[t, f] + value) - (east * lon + north * around(first_buf, t, f))
            out_ref[f, :, t, :] = jnp.where(keep, second, 0.0)


def per_device(spectral, modes_in, modes_out, mode_depth, legendre, wave_map, row_points):
    lev_rows, slots, fields, _, degrees = spectral.shape
    groups, shards = lax.axis_size("lev"), lax.axis_size("wave")
    lat_total = legendre.shape[2]
    lat_rows = lat_total // shards
    everyone, halo_rows = groups * shards, 8
    part_slots = slots // groups
    rows = 2 * shards * slots
    fits = slots == 2 * groups and 2 * degrees == 128 and lat_rows == 4
    fits = fits and lev_rows == 32 and everyone == 32 and rows == 128
    if not fits:
        return general_path(spectral, modes_in, modes_out, mode_depth, legendre, wave_map, row_points)
    norm = 1.0 / math.sqrt(shards * slots)
    exact = math.frexp(norm)[0] == 0.5
    columns = part_slots * fields * 2 * degrees
    modes = modes_in.shape[0]
    x = spectral.reshape(lev_rows, groups * columns)
    dims = (groups, shards, slots, lev_rows, fields, degrees, lat_total, norm if exact else 1.0)
    vmem = pl.BlockSpec(memory_space=pltpu.VMEM)
    hbm = pl.BlockSpec(memory_space=pltpu.HBM)
    message = fields * halo_rows
    bf16 = jnp.bfloat16
    bands, table, slope, limit = pl.pallas_call(
        functools.partial(exchange_kernel, dims),
        out_shape=(
            jax.ShapeDtypeStruct((halo_rows, fields, lev_rows, rows), bf16),
            jax.ShapeDtypeStruct((rows, LON), bf16),
            jax.ShapeDtypeStruct((2 * rows, LON), bf16),
            jax.ShapeDtypeStruct((8, 128), jnp.int32),
        ),
        in_specs=[hbm] * 7,
        out_specs=(vmem, hbm, hbm, hbm),
        scratch_shapes=[
            pltpu.VMEM((rows, LON), bf16),
            pltpu.VMEM((2 * rows, LON), bf16),
            pltpu.VMEM((8, 128), jnp.int32),
            pltpu.VMEM((modes, modes), bf16),
            pltpu.VMEM((modes, modes), bf16),
            pltpu.VMEM((1, modes), jnp.float32),
            pltpu.VMEM((part_slots, lat_total, degrees), bf16),
            pltpu.VMEM((1, shards * slots), jnp.int32),
            pltpu.VMEM((1, lat_rows), jnp.int32),
            pltpu.VMEM((groups, lev_rows, columns), bf16),
            pltpu.VMEM((groups, lev_rows, columns), bf16),
            pltpu.VMEM((everyone, message, rows), bf16),
            pltpu.VMEM((everyone, message, rows), bf16),
            pltpu.VMEM((everyone * message, rows), jnp.float32),
            pltpu.SemaphoreType.DMA((6,)),
            pltpu.SemaphoreType.DMA((3,)),
            pltpu.SemaphoreType.DMA((2,)),
            pltpu.SemaphoreType.DMA((groups,)),
            pltpu.SemaphoreType.DMA((groups,)),
            pltpu.SemaphoreType.DMA((everyone,)),
            pltpu.SemaphoreType.DMA((everyone,)),
        ],
        compiler_params=pltpu.CompilerParams(
            collective_id=0, has_side_effects=True, vmem_limit_bytes=60 * 1024 * 1024
        ),
        name="exchange",
    )(
        x, modes_in, modes_out, mode_depth.reshape(1, -1), jnp.swapaxes(legendre, 1, 2),
        wave_map.reshape(1, -1), row_points.reshape(1, -1),
    )
    chunk = 8
    return pl.pallas_call(
        functools.partial(section_kernel, None if exact else norm),
        grid=(lev_rows // chunk,),
        out_shape=jax.ShapeDtypeStruct((fields, lev_rows, lat_rows, LON), jnp.float32),
        in_specs=[
            pl.BlockSpec((8, 128), lambda i: (0, 0)),
            pl.BlockSpec((halo_rows, fields, chunk, rows), lambda i: (0, 0, i, 0)),
            pl.BlockSpec((rows, LON), lambda i: (0, 0)),
            pl.BlockSpec((2 * rows, LON), lambda i: (0, 0)),
        ],
        out_specs=pl.BlockSpec((fields, chunk, lat_rows, LON), lambda i: (0, i, 0, 0)),
        scratch_shapes=[pltpu.VMEM((halo_rows, fields, chunk, LON), jnp.float32)] * 3,
        compiler_params=pltpu.CompilerParams(vmem_limit_bytes=60 * 1024 * 1024),
        name="sections",
    )(limit, bands, table, slope)


def solution(mesh):
    in_specs = (
        P("lev", "wave", None, None, None),
        P(),
        P(),
        P(),
        P("wave", None, None),
        P(),
        P("wave"),
    )
    out_specs = P(None, "lev", "wave", None)
    return jax.shard_map(
        per_device, mesh=mesh, in_specs=in_specs, out_specs=out_specs, check_vma=False
    )
```
